32 devices in a mesh: expert: 4 (over y, x), hidden: 8 (over z, core).
Axes of the slice: x: 2, y: 2, z: 4, core: 2. Of those that a mesh axis runs over, the one named last changes fastest.
Arguments:
- layer_input: bfloat16 [1024, 4096], P('expert', 'hidden'), may hold values from -6 to 6
- output_grad: bfloat16 [1024, 4096], P('expert', 'hidden'), may hold values from -1.5 to 1.5
- latent_saved: bfloat16 [1024, 1024], P('expert'), may hold values from -6 to 6
- combined_saved: bfloat16 [1024, 1024], P('expert'), may hold values from -6 to 6
- expert_ids: int32 [1024, 22], P('expert'), may hold values from 0 to 511, as said below
- gate_values: bfloat16 [1024, 22], P('expert'), may hold values from 0.099609375 to 1.5
- down_proj: bfloat16 [1024, 4096], P(None, 'hidden'), may hold values from -0.09375 to 0.09375
- up_proj: bfloat16 [1024, 4096], P(None, 'hidden'), may hold values from -0.1875 to 0.1875
- expert_in: bfloat16 [4, 1024, 2688], P('expert', None, 'hidden'), may hold values from -0.1875 to 0.1875
- expert_out: bfloat16 [4, 2688, 1024], P('expert', 'hidden'), may hold values from -0.125 to 0.125
Outputs:
- input_grad: bfloat16 [1024, 4096], P('expert', 'hidden')
- down_grad: float32 [1024, 4096], P('expert', 'hidden')
- up_grad: float32 [1024, 4096], P('expert', 'hidden')
- gate_grad: float32 [1024, 22], P('expert')
- expert_in_grad: float32 [4, 1024, 2688], P('expert', None, 'hidden')
- expert_out_grad: float32 [4, 2688, 1024], P('expert', 'hidden')
The draws below stay inside these ranges and needn't reach their ends.
Inputs may be any that keep to these rules, and one draw needn't show every extreme that they name: `expert_ids`: each row names 22 different experts. In each aligned block of 256 rows (the rows of one index of the expert axis) each expert below 4 is named by at most 24 rows; some expert below 4 is named by exactly 24 rows in every block.
All inputs are finite; a program needn't handle non-finite values.
Results may differ from the reference program's by a relative error of at most 0.0065.
Values may be sent and summed in bfloat16 or wider, within the bound.
A program may use at most 64 MiB of HBM per device.

```python
import math
import jax
import jax.numpy as jnp
from jax import lax

D = 4096
LATENT = 1024
FF = 2688
EXPERTS = 512
TOPK = 22
TOK_DEV = 256
TOKENS = 1024
LIVE = 4
CAP = 24
N_EXPERT = 4


def draw_expert_ids(key, part):
    keys = jax.random.split(key, 8)
    blocks = TOKENS // TOK_DEV
    experts = jnp.arange(LIVE, dtype=jnp.int32)
    popular = jax.random.randint(keys[0], (LIVE,), 1, 5)
    counts = jax.random.randint(keys[1], (blocks, LIVE), 0, CAP + 1) * popular[None, :] // 4
    counts = jnp.minimum(counts, CAP)
    always_full = jax.random.randint(keys[2], (), 0, LIVE)
    extra_full = jax.random.randint(keys[3], (blocks,), 0, LIVE)
    at_limit = (experts[None, :] == always_full) | (experts[None, :] == extra_full[:, None])
    counts = jnp.where(at_limit, CAP, counts).astype(jnp.int32)
    scores = jax.random.randint(keys[4], (blocks, LIVE), 0, LIVE) * LIVE + experts[None, :]
    order = jnp.argsort(scores, axis=1).astype(jnp.int32)
    ordered = jnp.take_along_axis(counts, order, axis=1)
    starts_ordered = jnp.cumsum(ordered, axis=1) - ordered
    inverse = jnp.argsort(order, axis=1).astype(jnp.int32)
    starts = jnp.take_along_axis(starts_ordered, inverse, axis=1)
    token_iota = jnp.arange(TOK_DEV, dtype=jnp.int32)
    token_scores = jax.random.randint(keys[5], (blocks, TOK_DEV), 0, TOK_DEV) * TOK_DEV + token_iota[None, :]
    place = jnp.argsort(token_scores, axis=1).astype(jnp.int32)
    chosen = (jnp.mod(place[:, :, None] - starts[:, None, :], TOK_DEV) < counts[:, None, :]).astype(jnp.int32)
    chosen = chosen.reshape(TOKENS, LIVE)
    many = jnp.sum(chosen, axis=1)
    order_rank = jnp.cumsum(chosen, axis=1) - chosen
    shift_by = jax.random.randint(keys[6], (TOKENS,), 0, TOPK)
    begin_at = jax.random.randint(keys[7], (TOKENS,), 0, EXPERTS - LIVE)
    column = jnp.mod(jnp.arange(TOPK, dtype=jnp.int32)[None, :] - shift_by[:, None], TOPK)
    hit_table = chosen[:, None, :] * (order_rank[:, None, :] == column[:, :, None]).astype(jnp.int32)
    live_pick = jnp.sum(hit_table * experts[None, None, :], axis=2)
    other_pick = LIVE + jnp.mod(begin_at[:, None] + column - many[:, None], EXPERTS - LIVE)
    return jnp.where(column < many[:, None], live_pick, other_pick).astype(jnp.int32)


def levels(own_key, dims, pieces, low, high):
    def one(position, shards_of):
        draws = jax.random.uniform(jax.random.fold_in(jax.random.fold_in(own_key, 6), position), (shards_of,), jnp.float32, low / len(pieces), high / len(pieces))
        return jnp.repeat(jnp.exp(draws), dims[position] // shards_of).reshape((-1,) + (1,) * (len(dims) - position - 1))

    loudness = one(*pieces[0])
    for cut in pieces[1:]:
        loudness = loudness * one(*cut)
    return loudness


def bell_draw(own_key, dims, deviation, reach, shards=(), kind=jnp.bfloat16):
    drawn = jax.random.normal(own_key, dims, jnp.float32) * deviation
    if len(shards) > 0:
        drawn = levels(own_key, dims, shards, -0.22, 0.18) * drawn
    return jnp.clip(drawn, min=-reach, max=reach).astype(kind)


def setup_inputs(seed: int = 0) -> dict:
    key_list = jax.random.split(jax.random.key(seed), 11)
    return {
        "layer_input": bell_draw(key_list[0], (TOKENS, D), 1.0, 6.0, ((0, 4), (1, 8))),
        "output_grad": bell_draw(key_list[1], (TOKENS, D), 0.25, 1.5, ((0, 4), (1, 8))),
        "latent_saved": bell_draw(key_list[2], (TOKENS, LATENT), 1.0, 6.0, ((0, 4),)),
        "combined_saved": bell_draw(key_list[3], (TOKENS, LATENT), 1.0, 6.0, ((0, 4),)),
        "expert_ids": draw_expert_ids(jax.random.fold_in(key_list[10], 71), 0),
        "gate_values": jnp.clip(jnp.exp(math.log(1.5) - 2.7119641 * jax.random.uniform(key_list[5], (TOKENS, TOPK), jnp.float32) ** levels(key_list[5], (TOKENS, TOPK), ((0, 4),), -0.2, 0.2)), 0.099609375, 1.5).astype(jnp.bfloat16),
        "down_proj": bell_draw(key_list[6], (LATENT, D), D ** -0.5, 0.09375, ((1, 8),)),
        "up_proj": bell_draw(key_list[7], (LATENT, D), LATENT ** -0.5, 0.1875, ((1, 8),)),
        "expert_in": bell_draw(key_list[8], (LIVE, LATENT, FF), LATENT ** -0.5, 0.1875, ((0, 4), (2, 8))),
        "expert_out": bell_draw(key_list[9], (LIVE, FF, LATENT), FF ** -0.5, 0.125, ((0, 4), (1, 8))),
    }


def reference(layer_input, output_grad, latent_saved, combined_saved, expert_ids, gate_values, down_proj, up_proj, expert_in, expert_out):
    latent_cot = jnp.dot(output_grad, up_proj.T, preferred_element_type=jnp.float32).astype(jnp.bfloat16)
    up_grad = jnp.dot(combined_saved.T, output_grad, preferred_element_type=jnp.float32)
    gates = gate_values.astype(jnp.float32)
    row_limit = N_EXPERT * CAP

    def expert_step(running, inputs):
        latent_grad, gate_grad = running
        expert, first, second = inputs
        chosen = expert_ids == expert
        routed = jnp.any(chosen, axis=1)
        gate_token = jnp.sum(jnp.where(chosen, gates, jnp.zeros_like(gates)), axis=1)
        row_index = jnp.nonzero(routed, size=row_limit, fill_value=0)[0].astype(jnp.int32)
        filled = (jnp.arange(row_limit, dtype=jnp.int32) < jnp.sum(routed.astype(jnp.int32))).astype(jnp.float32)
        latent_rows = latent_saved[row_index]
        grad_rows = latent_cot[row_index]
        gate_rows = gate_token[row_index] * filled
        pre_act = jnp.dot(latent_rows, first, preferred_element_type=jnp.float32)
        relu_out = jnp.maximum(pre_act, 0.0)
        back_proj = jnp.dot(grad_rows, second.T, preferred_element_type=jnp.float32)
        gate_back = jnp.sum(back_proj * relu_out * relu_out, axis=1) * filled
        scaled_act = (gate_rows[:, None] * relu_out * relu_out).astype(jnp.bfloat16)
        pre_grad = (2.0 * gate_rows[:, None] * relu_out * back_proj).astype(jnp.bfloat16)
        grad_second = jnp.dot(scaled_act.T, grad_rows, preferred_element_type=jnp.float32)
        grad_first = jnp.dot(latent_rows.T, pre_grad, preferred_element_type=jnp.float32)
        latent_back = jnp.dot(pre_grad, first.T, preferred_element_type=jnp.float32)
        latent_grad = latent_grad.at[row_index].add(latent_back * filled[:, None])
        token_gate = jnp.zeros((TOKENS,), jnp.float32).at[row_index].add(gate_back)
        gate_grad = gate_grad + jnp.where(chosen, token_gate[:, None], jnp.zeros_like(gate_grad))
        return (latent_grad, gate_grad), (grad_first, grad_second)

    start = (jnp.zeros((TOKENS, LATENT), jnp.float32), jnp.zeros((TOKENS, TOPK), jnp.float32))
    (latent_grad, gate_grad), (expert_in_grad, expert_out_grad) = lax.scan(
        expert_step, start, (jnp.arange(LIVE, dtype=jnp.int32), expert_in, expert_out))
    latent_bf = latent_grad.astype(jnp.bfloat16)
    input_grad = jnp.dot(latent_bf, down_proj, preferred_element_type=jnp.float32).astype(jnp.bfloat16)
    down_grad = jnp.dot(latent_bf.T, layer_input, preferred_element_type=jnp.float32)
    return input_grad, down_grad, up_grad, gate_grad, expert_in_grad, expert_out_grad
```

```python
import functools

import jax
import jax.numpy as jnp
from jax import lax
from jax.experimental import pallas as pl
from jax.experimental.pallas import tpu as pltpu
from jax.sharding import PartitionSpec as P

F32 = jnp.float32
BF16 = jnp.bfloat16
LANES = 128
ROWS = 16


def mm(a, b, ca, cb):
    return lax.dot_general(a, b, (((ca,), (cb,)), ((), ())), preferred_element_type=F32)


def rows_at(index, size):
    return pl.ds(pl.multiple_of(index * size, size), size)


def fused_kernel(
    groups,
    shares,
    pad,
    x_ref,
    og_ref,
    z_ref,
    u_ref,
    ids_ref,
    gates_ref,
    down_ref,
    up_ref,
    ein_ref,
    eout_ref,
    ig_ref,
    dg_ref,
    ug_ref,
    gg_ref,
    eig_ref,
    eog_ref,
    dt_s,
    og_s,
    og_r,
    z_s,
    z_r,
    x_s,
    x_r,
    up_s,
    up_r,
    cf,
    cs,
    cr,
    cag,
    bf,
    bs,
    br,
    bag,
    home,
    dn,
    sems_e,
    sems_h,
):
    e = lax.axis_index("expert")
    h = lax.axis_index("hidden")
    tokens, topk = ids_ref.shape
    slots = groups * pad
    latent = z_ref.shape[1]
    block = slots // shares
    lw = latent // groups

    def expert_peer(j):
        return lax.rem(e + j, groups)

    def hidden_peer(j):
        return lax.rem(h + j, shares)

    def expert_source(j):
        return lax.rem(e + (groups - j), groups)

    def hidden_source(j):
        return lax.rem(h + (shares - j), shares)

    def to_expert(phase, j, src, dst):
        copy = pltpu.make_async_remote_copy(
            src_ref=src,
            dst_ref=dst,
            send_sem=sems_e.at[phase, 0, j],
            recv_sem=sems_e.at[phase, 1, j],
            device_id=(expert_peer(j), h),
            device_id_type=pl.DeviceIdType.MESH,
        )
        copy.start()
        return copy

    def to_hidden(phase, j, src, dst):
        copy = pltpu.make_async_remote_copy(
            src_ref=src,
            dst_ref=dst,
            send_sem=sems_h.at[phase, 0, j],
            recv_sem=sems_h.at[phase, 1, j],
            device_id=(e, hidden_peer(j)),
            device_id_type=pl.DeviceIdType.MESH,
        )
        copy.start()
        return copy

    barrier = pltpu.get_barrier_semaphore()
    for j in range(1, groups):
        pl.semaphore_signal(
            barrier,
            inc=1,
            device_id=(expert_peer(j), h),
            device_id_type=pl.DeviceIdType.MESH,
        )
    for j in range(1, shares):
        pl.semaphore_signal(
            barrier,
            inc=1,
            device_id=(e, hidden_peer(j)),
            device_id_type=pl.DeviceIdType.MESH,
        )

    ids = ids_ref[...]
    gates = gates_ref[...].astype(F32)
    lane = lax.broadcasted_iota(jnp.int32, (tokens, slots), 1)
    lane_expert = lane // pad
    member = jnp.zeros((tokens, slots), F32)
    gate_token = jnp.zeros((tokens, slots), F32)
    for k in range(topk):
        hit = ids[:, k : k + 1] == lane_expert
        member = jnp.where(hit, 1.0, member)
        gate_token = jnp.where(hit, gates[:, k : k + 1], gate_token)
    row_t = lax.broadcasted_iota(jnp.int32, (tokens, tokens), 0)
    col_t = lax.broadcasted_iota(jnp.int32, (tokens, tokens), 1)
    earlier = jnp.where(col_t < row_t, 1.0, 0.0).astype(BF16)
    before = mm(earlier, member.astype(BF16), 1, 0)
    rank = (lane - lane_expert * pad).astype(F32)
    disp_t = jnp.where(before == rank, member, 0.0)
    disp = disp_t.T.astype(BF16)
    dt_s[...] = disp_t.astype(BF16)

    og_s[...] = mm(disp, og_ref[...], 1, 0).astype(BF16).reshape(og_s.shape)
    pl.semaphore_wait(barrier, groups + shares - 2)
    og_c = [
        to_expert(0, j, og_s.at[expert_peer(j)], og_r.at[e]) for j in range(1, groups)
    ]
    z_s[:, :, 0:latent] = mm(disp, z_ref[...], 1, 0).astype(BF16).reshape(groups, pad, latent)
    gate_all = mm(disp, gate_token.astype(BF16), 1, 0)
    srow = lax.broadcasted_iota(jnp.int32, (slots, slots), 0)
    scol = lax.broadcasted_iota(jnp.int32, (slots, slots), 1)
    gate_col = jnp.sum(
        jnp.where(scol == (srow // pad) * pad, gate_all, 0.0), axis=1, keepdims=True
    )
    z_s[:, :, latent : latent + LANES] = (
        jnp.broadcast_to(gate_col, (slots, LANES)).astype(BF16).reshape(groups, pad, LANES)
    )
    z_c = [to_expert(1, j, z_s.at[expert_peer(j)], z_r.at[e]) for j in range(1, groups)]
    og_r[e] = og_s[e]
    z_r[e] = z_s[e]
    x_s[...] = mm(disp, x_ref[...], 1, 0).astype(BF16).reshape(x_s.shape)
    x_r[:, rows_at(e, pad), :] = x_s[...]
    for j in range(1, groups):
        up_s[j - 1] = mm(
            u_ref[:, rows_at(expert_peer(j), lw)], og_ref[...], 0, 0
        ).astype(BF16)
    ug_ref[...] = mm(u_ref[:, rows_at(e, lw)], og_ref[...], 0, 0)

    for c in og_c:
        c.wait_recv()
    cot_part = mm(og_r[...].reshape(slots, og_ref.shape[1]), up_ref[...], 1, 1)
    cs[...] = cot_part.astype(BF16)
    cf[...] = cot_part
    crs = [
        to_hidden(0, j, cs.at[rows_at(hidden_peer(j), block)], cr.at[h])
        for j in range(1, shares)
    ]
    for c in z_c:
        c.wait_recv()
    x_c = [
        to_expert(2, j, x_s, x_r.at[:, rows_at(e, pad), :]) for j in range(1, groups)
    ]
    up_c = [to_expert(3, j, up_s.at[j - 1], up_r.at[j - 1]) for j in range(1, groups)]
    zb = z_r[:, :, 0:latent].reshape(slots, latent)
    gate_b = z_r[:, :, latent : latent + LANES].astype(F32).reshape(slots, LANES)[:, 0:1]
    act = jnp.maximum(mm(zb, ein_ref[...], 1, 0), 0.0)
    square = act * act
    scaled = (gate_b * square).astype(BF16)
    cot = cf[rows_at(h, block), :]
    for j in range(1, shares):
        crs[j - 1].wait_recv()
        cot = cot + cr[hidden_source(j)].astype(F32)
    cag[rows_at(h, block), :] = cot.astype(BF16)
    cagc = [
        to_hidden(1, j, cag.at[rows_at(h, block)], cag.at[rows_at(h, block)])
        for j in range(1, shares)
    ]
    for c in cagc:
        c.wait_recv()

    cotb = cag[...]
    back = mm(cotb, eout_ref[...], 1, 1)
    gate_part = jnp.sum(back * square, axis=1, keepdims=True)
    pre_grad = ((2.0 * gate_b) * act * back).astype(BF16)
    part = mm(pre_grad, ein_ref[...], 1, 1)
    gate_wide = jnp.broadcast_to(gate_part, (slots, LANES))
    bf[:, 0:latent] = part
    bf[:, latent : latent + LANES] = gate_wide
    bs[:, 0:latent] = part.astype(BF16)
    bs[:, latent : latent + LANES] = gate_wide.astype(BF16)
    brs = [
        to_hidden(2, j, bs.at[rows_at(hidden_peer(j), block)], br.at[h])
        for j in range(1, shares)
    ]
    eog_ref[0] = mm(scaled, cotb, 0, 0)
    eig_ref[0] = mm(zb, pre_grad, 0, 0)
    total = bf[rows_at(h, block), :]
    for j in range(1, shares):
        brs[j - 1].wait_recv()
        total = total + br[hidden_source(j)].astype(F32)
    bag[rows_at(h, block), :] = total.astype(BF16)
    bagc = [
        to_hidden(3, j, bag.at[rows_at(h, block)], bag.at[rows_at(h, block)])
        for j in range(1, shares)
    ]
    for j in range(1, groups):
        up_c[j - 1].wait_recv()
        ug_ref[...] += up_r[j - 1].astype(F32)
    for c in x_c:
        c.wait_recv()
    for c in bagc:
        c.wait_recv()

    home_c = [
        to_expert(4, j, bag.at[rows_at(expert_peer(j), pad)], home.at[rows_at(e, pad)])
        for j in range(1, groups)
    ]
    dn_c = [
        to_expert(5, j, bag.at[:, rows_at(expert_peer(j), lw)], dn.at[e])
        for j in range(1, groups)
    ]
    home[rows_at(e, pad), :] = bag[rows_at(e, pad), :]
    dn[e] = bag[:, rows_at(e, lw)]
    for c in home_c:
        c.wait_recv()
    disp_home = dt_s[...]
    latent_grad = mm(disp_home, home[:, 0:latent], 1, 0).astype(BF16)
    ig_ref[...] = mm(latent_grad, down_ref[...], 1, 0).astype(BF16)
    gate_rows = home[:, latent : latent + LANES].astype(F32)
    wrow = lax.broadcasted_iota(jnp.int32, (slots, LANES), 0)
    wcol = lax.broadcasted_iota(jnp.int32, (slots, LANES), 1)
    gate_mat = jnp.where(wcol == wrow // pad, gate_rows, 0.0).astype(BF16)
    gate_by = mm(disp_home, gate_mat, 1, 0)
    gate_out = jnp.zeros((tokens, topk), F32)
    for n in range(groups):
        gate_out = jnp.where(ids == n, gate_by[:, n : n + 1], gate_out)
    gg_ref[...] = gate_out
    for c in dn_c:
        c.wait_recv()
    dg_ref[...] = mm(
        dn[...].reshape(groups * slots, lw),
        x_r[...].reshape(groups * slots, x_ref.shape[1]),
        0,
        0,
    )
    for c in og_c + z_c + crs + x_c + up_c + cagc + brs + bagc + home_c + dn_c:
        c.wait_send()


def fused(
    layer_input,
    output_grad,
    latent_saved,
    combined_saved,
    expert_ids,
    gate_values,
    down_proj,
    up_proj,
    expert_in,
    expert_out,
):
    groups = lax.axis_size("expert")
    shares = lax.axis_size("hidden")
    tokens, width = layer_input.shape
    latent = latent_saved.shape[1]
    ff = expert_in.shape[2]
    pad = padded_rows(tokens)
    slots = groups * pad
    block = slots // shares
    wide = latent + LANES
    lw = latent // groups
    vmem = pl.BlockSpec(memory_space=pltpu.VMEM)
    return pl.pallas_call(
        functools.partial(fused_kernel, groups, shares, pad),
        out_shape=(
            jax.ShapeDtypeStruct((tokens, width), BF16),
            jax.ShapeDtypeStruct((lw, width), F32),
            jax.ShapeDtypeStruct((lw, width), F32),
            jax.ShapeDtypeStruct(expert_ids.shape, F32),
            jax.ShapeDtypeStruct(expert_in.shape, F32),
            jax.ShapeDtypeStruct(expert_out.shape, F32),
        ),
        in_specs=[vmem] * 10,
        out_specs=[vmem] * 6,
        scratch_shapes=[
            pltpu.VMEM((tokens, slots), BF16),
            pltpu.VMEM((groups, pad, width), BF16),
            pltpu.VMEM((groups, pad, width), BF16),
            pltpu.VMEM((groups, pad, wide), BF16),
            pltpu.VMEM((groups, pad, wide), BF16),
            pltpu.VMEM((groups, pad, width), BF16),
            pltpu.VMEM((groups, slots, width), BF16),
            pltpu.VMEM((groups - 1, lw, width), BF16),
            pltpu.VMEM((groups - 1, lw, width), BF16),
            pltpu.VMEM((slots, latent), F32),
            pltpu.VMEM((slots, latent), BF16),
            pltpu.VMEM((shares, block, latent), BF16),
            pltpu.VMEM((slots, latent), BF16),
            pltpu.VMEM((slots, wide), F32),
            pltpu.VMEM((slots, wide), BF16),
            pltpu.VMEM((shares, block, wide), BF16),
            pltpu.VMEM((slots, wide), BF16),
            pltpu.VMEM((slots, wide), BF16),
            pltpu.VMEM((groups, slots, lw), BF16),
            pltpu.SemaphoreType.DMA((6, 2, groups)),
            pltpu.SemaphoreType.DMA((4, 2, shares)),
        ],
        compiler_params=pltpu.CompilerParams(
            collective_id=0, has_side_effects=True, vmem_limit_bytes=48 * 1024 * 1024
        ),
    )(
        layer_input,
        output_grad,
        latent_saved,
        combined_saved,
        expert_ids,
        gate_values,
        down_proj,
        up_proj,
        expert_in[0],
        expert_out[0],
    )


def padded_rows(tokens):
    return -(-(tokens * 3 // 32) // ROWS) * ROWS


def fits(layer_input, latent_saved, expert_in):
    groups = lax.axis_size("expert")
    shares = lax.axis_size("hidden")
    slots = groups * padded_rows(layer_input.shape[0])
    return (
        expert_in.shape[0] == 1
        and slots % (ROWS * shares) == 0
        and slots % LANES == 0
        and latent_saved.shape[1] % (LANES * groups) == 0
        and layer_input.shape[1] % LANES == 0
    )


def per_device(*arrays):
    run = fused if fits(arrays[0], arrays[2], arrays[8]) else on_device
    return run(*arrays)


def slot_layout(table, groups, local_count):
    tokens_here = table.shape[0]
    return table.T.reshape(groups, local_count, tokens_here).transpose(1, 0, 2)[:, :, None, :]


def on_device(
    layer_input,
    output_grad,
    latent_saved,
    combined_saved,
    expert_ids,
    gate_values,
    down_proj,
    up_proj,
    expert_in,
    expert_out,
):
    groups = lax.axis_size("expert")
    shares = lax.axis_size("hidden")
    tokens_here = layer_input.shape[0]
    latent_width = latent_saved.shape[1]
    local_count = expert_in.shape[0]
    capacity = tokens_here * 3 // 32
    live_count = local_count * groups
    slot_total = local_count * groups * capacity
    part_width = latent_width // shares
    partial_cot = jnp.einsum("td,ld->tl", output_grad, up_proj, preferred_element_type=jnp.float32)
    member = expert_ids[:, :, None] == jnp.arange(live_count, dtype=jnp.int32)[None, None, :]
    per_token = jnp.sum(member.astype(jnp.int32), axis=1)
    token_iota = jnp.arange(tokens_here, dtype=jnp.int32)
    earlier = (token_iota[None, :] < token_iota[:, None]).astype(jnp.bfloat16)
    before = jnp.dot(
        earlier, per_token.astype(jnp.bfloat16), preferred_element_type=jnp.float32
    ).astype(jnp.int32)
    gate_token = jnp.sum(
        jnp.where(member, gate_values.astype(jnp.float32)[:, :, None], 0.0), axis=1
    )
    rank_iota = jnp.arange(capacity, dtype=jnp.int32)[None, None, :, None]
    hit_slot = (slot_layout(per_token, groups, local_count) == 1) & (
        slot_layout(before, groups, local_count) == rank_iota
    )
    gate_slot = jnp.sum(
        jnp.where(hit_slot, slot_layout(gate_token, groups, local_count), 0.0), axis=3
    )
    gate_send = gate_slot.astype(jnp.bfloat16)
    dispatch_bf = hit_slot.astype(jnp.bfloat16).reshape(slot_total, tokens_here)
    cot_part = lax.psum_scatter(partial_cot, "hidden", scatter_dimension=1, tiled=True).astype(
        jnp.bfloat16
    )
    latent_part = lax.dynamic_slice_in_dim(
        latent_saved, lax.axis_index("hidden") * part_width, part_width, 1
    )
    cot_rows = jnp.dot(dispatch_bf, cot_part, preferred_element_type=jnp.float32).astype(
        jnp.bfloat16
    )
    latent_rows = jnp.dot(dispatch_bf, latent_part, preferred_element_type=jnp.float32).astype(
        jnp.bfloat16
    )
    cot_piece, latent_piece, gate_recv = (
        lax.all_to_all(
            cot_rows.reshape(local_count, groups, capacity, part_width),
            "expert",
            split_axis=1,
            concat_axis=1,
            tiled=True,
        ),
        lax.all_to_all(
            latent_rows.reshape(local_count, groups, capacity, part_width),
            "expert",
            split_axis=1,
            concat_axis=1,
            tiled=True,
        ),
        lax.all_to_all(gate_send, "expert", split_axis=1, concat_axis=1, tiled=True),
    )
    cot_recv, latent_recv = (
        lax.all_gather(cot_piece, "hidden", axis=3, tiled=True),
        lax.all_gather(latent_piece, "hidden", axis=3, tiled=True),
    )
    row_count = groups * capacity
    cot_block = cot_recv.reshape(local_count, row_count, latent_width)
    latent_block = latent_recv.reshape(local_count, row_count, latent_width)
    gate_block = gate_recv.reshape(local_count, row_count).astype(jnp.float32)
    pre_act = jnp.einsum(
        "erl,elf->erf", latent_block, expert_in, preferred_element_type=jnp.float32
    )
    relu_out = jnp.maximum(pre_act, 0.0)
    back_proj = jnp.einsum(
        "erl,efl->erf", cot_block, expert_out, preferred_element_type=jnp.float32
    )
    gate_part = jnp.sum(back_proj * relu_out * relu_out, axis=2)
    scaled_act = (gate_block[:, :, None] * relu_out * relu_out).astype(jnp.bfloat16)
    pre_grad = (2.0 * gate_block[:, :, None] * relu_out * back_proj).astype(jnp.bfloat16)
    expert_out_grad = jnp.einsum(
        "erf,erl->efl", scaled_act, cot_block, preferred_element_type=jnp.float32
    )
    expert_in_grad = jnp.einsum(
        "erl,erf->elf", latent_block, pre_grad, preferred_element_type=jnp.float32
    )
    latent_back = jnp.einsum(
        "erf,elf->erl", pre_grad, expert_in, preferred_element_type=jnp.float32
    )
    latent_back = latent_back.reshape(local_count, groups, capacity, latent_width)
    gate_part = gate_part.reshape(local_count, groups, capacity)
    dispatch_full = hit_slot.astype(jnp.float32)
    dispatch_flat = dispatch_full.reshape(slot_total, tokens_here)
    rows_home, gate_home = (
        lax.all_to_all(latent_back, "expert", split_axis=1, concat_axis=1, tiled=True),
        lax.all_to_all(gate_part, "expert", split_axis=1, concat_axis=1, tiled=True),
    )
    token_sums = jnp.dot(
        dispatch_flat.T,
        rows_home.reshape(slot_total, latent_width),
        precision=lax.Precision.HIGHEST,
        preferred_element_type=jnp.float32,
    )
    by_expert = jnp.sum(dispatch_full * gate_home[:, :, :, None], axis=2)
    by_expert = by_expert.transpose(2, 1, 0).reshape(tokens_here, live_count)
    gate_local = jnp.sum(jnp.where(member, by_expert[:, None, :], 0.0), axis=2)
    latent_grad, gate_grad = lax.psum((token_sums, gate_local), "hidden")
    latent_bf = latent_grad.astype(jnp.bfloat16)
    input_grad = jnp.dot(latent_bf, down_proj, preferred_element_type=jnp.float32).astype(
        jnp.bfloat16
    )
    down_term = jnp.einsum("tl,td->ld", latent_bf, layer_input, preferred_element_type=jnp.float32)
    up_term = jnp.einsum(
        "tl,td->ld", combined_saved, output_grad, preferred_element_type=jnp.float32
    )
    down_grad, up_grad = (
        lax.psum_scatter(down_term, "expert", scatter_dimension=0, tiled=True),
        lax.psum_scatter(up_term, "expert", scatter_dimension=0, tiled=True),
    )
    return (input_grad, down_grad, up_grad, gate_grad, expert_in_grad, expert_out_grad)


def solution(mesh):
    return jax.shard_map(
        per_device,
        mesh=mesh,
        in_specs=(
            P("expert", "hidden"),
            P("expert", "hidden"),
            P("expert", None),
            P("expert", None),
            P("expert", None),
            P("expert", None),
            P(None, "hidden"),
            P(None, "hidden"),
            P("expert", None, "hidden"),
            P("expert", "hidden", None),
        ),
        out_specs=(
            P("expert", "hidden"),
            P("expert", "hidden"),
            P("expert", "hidden"),
            P("expert", None),
            P("expert", None, "hidden"),
            P("expert", "hidden", None),
        ),
        check_vma=False,
    )
```

```python
import functools

import jax
import jax.numpy as jnp
from jax import lax
from jax.experimental import pallas as pl
from jax.experimental.pallas import tpu as pltpu
from jax.sharding import PartitionSpec as P

F32 = jnp.float32
BF16 = jnp.bfloat16
LANES = 128
ROWS = 16


def mm(a, b, ca, cb):
    return lax.dot_general(a, b, (((ca,), (cb,)), ((), ())), preferred_element_type=F32)


def rows_at(index, size):
    return pl.ds(pl.multiple_of(index * size, size), size)


def fused_kernel(
    groups,
    shares,
    pad,
    x_hbm,
    og_hbm,
    z_hbm,
    u_hbm,
    ids_hbm,
    gates_hbm,
    up_hbm,
    ein_hbm,
    eout_hbm,
    disp_ref,
    scaled_ref,
    pre_ref,
    zb_ref,
    cag,
    home,
    dn,
    x_r,
    ug_ref,
    x_ref,
    og_ref,
    z_ref,
    u_ref,
    ids_ref,
    gates_ref,
    up_ref,
    ein_ref,
    eout_ref,
    og_s,
    og_r,
    z_s,
    z_r,
    x_s,
    up_s,
    up_r,
    cf,
    cs,
    cr,
    bf,
    bs,
    br,
    bag,
    sems_in,
    sems_e,
    sems_h,
):
    e = lax.axis_index("expert")
    h = lax.axis_index("hidden")
    tokens = ids_ref.shape[1]
    slots = groups * pad
    latent = z_ref.shape[1]
    block = slots // shares
    lw = latent // groups

    def expert_peer(j):
        return lax.rem(e + j, groups)

    def hidden_peer(j):
        return lax.rem(h + j, shares)

    def expert_source(j):
        return lax.rem(e + (groups - j), groups)

    def hidden_source(j):
        return lax.rem(h + (shares - j), shares)

    def to_expert(phase, j, src, dst):
        copy = pltpu.make_async_remote_copy(
            src_ref=src,
            dst_ref=dst,
            send_sem=sems_e.at[phase, 0, j],
            recv_sem=sems_e.at[phase, 1, j],
            device_id=(expert_peer(j), h),
            device_id_type=pl.DeviceIdType.MESH,
        )
        copy.start()
        return copy

    def to_hidden(phase, j, src, dst):
        copy = pltpu.make_async_remote_copy(
            src_ref=src,
            dst_ref=dst,
            send_sem=sems_h.at[phase, 0, j],
            recv_sem=sems_h.at[phase, 1, j],
            device_id=(e, hidden_peer(j)),
            device_id_type=pl.DeviceIdType.MESH,
        )
        copy.start()
        return copy

    sources = (ids_hbm, gates_hbm, og_hbm, z_hbm, up_hbm, ein_hbm, x_hbm, u_hbm, eout_hbm)
    targets = (ids_ref, gates_ref, og_ref, z_ref, up_ref, ein_ref, x_ref, u_ref, eout_ref)
    loads = [
        pltpu.make_async_copy(src, dst, sems_in.at[n])
        for n, (src, dst) in enumerate(zip(sources, targets))
    ]
    for load in loads:
        load.start()
    ids_in, gates_in, og_in, z_in, up_in, ein_in, x_in, u_in, eout_in = loads

    barrier = pltpu.get_barrier_semaphore()
    for j in range(1, groups):
        pl.semaphore_signal(
            barrier,
            inc=1,
            device_id=(expert_peer(j), h),
            device_id_type=pl.DeviceIdType.MESH,
        )
    for j in range(1, shares):
        pl.semaphore_signal(
            barrier,
            inc=1,
            device_id=(e, hidden_peer(j)),
            device_id_type=pl.DeviceIdType.MESH,
        )

    row_t = lax.broadcasted_iota(jnp.int32, (tokens, tokens), 0)
    col_t = lax.broadcasted_iota(jnp.int32, (tokens, tokens), 1)
    earlier = jnp.where(row_t < col_t, 1.0, 0.0).astype(BF16)
    ids_in.wait()
    gates_in.wait()
    ids = ids_ref[...]
    gates = gates_ref[...].astype(F32)
    member_rows = []
    gate_rows = []
    for n in range(groups):
        hit = ids == n
        member_rows.append(jnp.sum(jnp.where(hit, 1.0, 0.0), axis=0, keepdims=True))
        gate_rows.append(jnp.sum(jnp.where(hit, gates, 0.0), axis=0, keepdims=True))
    member = jnp.concatenate(
        [jnp.broadcast_to(row, (pad, tokens)) for row in member_rows], axis=0
    )
    gate_token = jnp.concatenate(
        [jnp.broadcast_to(row, (pad, tokens)) for row in gate_rows], axis=0
    )
    before = mm(member.astype(BF16), earlier, 1, 0)
    slot = lax.broadcasted_iota(jnp.int32, (slots, tokens), 0)
    rank = lax.rem(slot, pad).astype(F32)
    chosen = jnp.where(before == rank, member, 0.0)
    disp = chosen.astype(BF16)
    disp_ref[...] = disp
    og_in.wait()

    og_s[...] = mm(disp, og_ref[...], 1, 0).astype(BF16).reshape(og_s.shape)
    pl.semaphore_wait(barrier, groups + shares - 2)
    og_c = [
        to_expert(0, j, og_s.at[expert_peer(j)], og_r.at[e]) for j in range(1, groups)
    ]
    z_in.wait()
    z_s[:, :, 0:latent] = mm(disp, z_ref[...], 1, 0).astype(BF16).reshape(groups, pad, latent)
    gate_col = jnp.sum(chosen * gate_token, axis=1, keepdims=True)
    z_s[:, :, latent : latent + LANES] = (
        jnp.broadcast_to(gate_col, (slots, LANES)).astype(BF16).reshape(groups, pad, LANES)
    )
    z_c = [to_expert(1, j, z_s.at[expert_peer(j)], z_r.at[e]) for j in range(1, groups)]
    og_r[e] = og_s[e]
    z_r[e] = z_s[e]
    x_in.wait()
    x_s[...] = mm(disp, x_ref[...], 1, 0).astype(BF16).reshape(x_s.shape)
    x_r[:, rows_at(e, pad), :] = x_s[...]
    u_in.wait()
    for j in range(1, groups):
        up_s[j - 1] = mm(
            u_ref[:, rows_at(expert_peer(j), lw)], og_ref[...], 0, 0
        ).astype(BF16)
    ug_ref[...] = mm(u_ref[:, rows_at(e, lw)], og_ref[...], 0, 0)

    for c in og_c:
        c.wait_recv()
    up_in.wait()
    cot_part = mm(og_r[...].reshape(slots, og_ref.shape[1]), up_ref[...], 1, 1)
    cs[...] = cot_part.astype(BF16)
    cf[...] = cot_part
    crs = [
        to_hidden(0, j, cs.at[rows_at(hidden_peer(j), block)], cr.at[h])
        for j in range(1, shares)
    ]
    for c in z_c:
        c.wait_recv()
    x_c = [
        to_expert(2, j, x_s, x_r.at[:, rows_at(e, pad), :]) for j in range(1, groups)
    ]
    up_c = [to_expert(3, j, up_s.at[j - 1], up_r.at[j - 1]) for j in range(1, groups)]
    zb = z_r[:, :, 0:latent].reshape(slots, latent)
    gate_b = z_r[:, :, latent : latent + LANES].astype(F32).reshape(slots, LANES)[:, 0:1]
    zb_ref[...] = zb
    ein_in.wait()
    act = jnp.maximum(mm(zb, ein_ref[...], 1, 1), 0.0)
    square = act * act
    scaled_ref[...] = (gate_b * square).astype(BF16)
    eout_in.wait()
    cot = cf[rows_at(h, block), :]
    for j in range(1, shares):
        crs[j - 1].wait_recv()
        cot = cot + cr[hidden_source(j)].astype(F32)
    cag[rows_at(h, block), :] = cot.astype(BF16)
    cagc = [
        to_hidden(1, j, cag.at[rows_at(h, block)], cag.at[rows_at(h, block)])
        for j in range(1, shares)
    ]
    for c in cagc:
        c.wait_recv()

    cotb = cag[...]
    back = mm(cotb, eout_ref[...], 1, 1)
    gate_part = jnp.sum(back * square, axis=1, keepdims=True)
    pre_grad = ((2.0 * gate_b) * act * back).astype(BF16)
    pre_ref[...] = pre_grad
    part = mm(pre_grad, ein_ref[...], 1, 0)
    gate_wide = jnp.broadcast_to(gate_part, (slots, LANES))
    bf[:, 0:latent] = part
    bf[:, latent : latent + LANES] = gate_wide
    bs[:, 0:latent] = part.astype(BF16)
    bs[:, latent : latent + LANES] = gate_wide.astype(BF16)
    brs = [
        to_hidden(2, j, bs.at[rows_at(hidden_peer(j), block)], br.at[h])
        for j in range(1, shares)
    ]
    total = bf[rows_at(h, block), :]
    for j in range(1, shares):
        brs[j - 1].wait_recv()
        total = total + br[hidden_source(j)].astype(F32)
    bag[rows_at(h, block), :] = total.astype(BF16)
    bagc = [
        to_hidden(3, j, bag.at[rows_at(h, block)], bag.at[rows_at(h, block)])
        for j in range(1, shares)
    ]
    for j in range(1, groups):
        up_c[j - 1].wait_recv()
        ug_ref[...] += up_r[j - 1].astype(F32)
    for c in x_c:
        c.wait_recv()
    for c in bagc:
        c.wait_recv()

    home_c = [
        to_expert(4, j, bag.at[rows_at(expert_peer(j), pad)], home.at[rows_at(e, pad)])
        for j in range(1, groups)
    ]
    dn_c = [
        to_expert(5, j, bag.at[:, rows_at(expert_peer(j), lw)], dn.at[e])
        for j in range(1, groups)
    ]
    home[rows_at(e, pad), :] = bag[rows_at(e, pad), :]
    dn[e] = bag[:, rows_at(e, lw)]
    for c in home_c + dn_c:
        c.wait_recv()
    for c in og_c + z_c + crs + x_c + up_c + cagc + brs + bagc + home_c + dn_c:
        c.wait_send()


def outputs_kernel(
    groups,
    pad,
    disp_ref,
    scaled_ref,
    pre_ref,
    zb_ref,
    cot_ref,
    home_ref,
    dn_ref,
    x_ref,
    ug_ref,
    ids_ref,
    down_ref,
    ig_hbm,
    dg_hbm,
    ug_hbm,
    gg_hbm,
    eig_hbm,
    eog_hbm,
    ig_v,
    dg_v,
    gg_v,
    eig_v,
    eog_v,
    sems,
):
    slots = groups * pad
    latent = cot_ref.shape[1]
    stores = []

    def store(src, dst):
        copy = pltpu.make_async_copy(src, dst, sems.at[len(stores)])
        copy.start()
        stores.append(copy)

    store(ug_ref, ug_hbm)
    eog_v[...] = mm(scaled_ref[...], cot_ref[...], 0, 0)
    store(eog_v, eog_hbm)
    eig_v[...] = mm(pre_ref[...], zb_ref[...], 0, 0)
    store(eig_v, eig_hbm)
    dg_v[...] = mm(
        dn_ref[...].reshape(groups * slots, dn_ref.shape[2]),
        x_ref[...].reshape(groups * slots, x_ref.shape[2]),
        0,
        0,
    )
    store(dg_v, dg_hbm)
    disp = disp_ref[...]
    latent_grad = mm(disp, home_ref[:, 0:latent], 0, 0).astype(BF16)
    ig_v[...] = mm(latent_grad, down_ref[...], 1, 0).astype(BF16)
    store(ig_v, ig_hbm)
    by_slot = home_ref[:, latent : latent + LANES].astype(F32)[:, 0:1] * disp.astype(F32)
    ids = ids_ref[...]
    gate_out = jnp.zeros(ids.shape, F32)
    for n in range(groups):
        by_token = jnp.sum(by_slot[n * pad : (n + 1) * pad], axis=0, keepdims=True)
        gate_out = jnp.where(ids == n, by_token, gate_out)
    gg_v[...] = gate_out
    store(gg_v, gg_hbm)
    for copy in stores:
        copy.wait()


def fused(
    layer_input,
    output_grad,
    latent_saved,
    combined_saved,
    expert_ids,
    gate_values,
    down_proj,
    up_proj,
    expert_in,
    expert_out,
):
    groups = lax.axis_size("expert")
    shares = lax.axis_size("hidden")
    tokens, width = layer_input.shape
    latent = latent_saved.shape[1]
    ff = expert_in.shape[2]
    pad = padded_rows(tokens)
    slots = groups * pad
    block = slots // shares
    wide = latent + LANES
    lw = latent // groups
    vmem = pl.BlockSpec(memory_space=pltpu.VMEM)
    hbm = pl.BlockSpec(memory_space=pltpu.HBM)
    ids_t = expert_ids.T
    ins = (
        layer_input,
        output_grad,
        latent_saved,
        combined_saved,
        ids_t,
        gate_values.T,
        up_proj,
        expert_in[0].T,
        expert_out[0],
    )
    between = pl.pallas_call(
        functools.partial(fused_kernel, groups, shares, pad),
        out_shape=(
            jax.ShapeDtypeStruct((slots, tokens), BF16),
            jax.ShapeDtypeStruct((slots, ff), BF16),
            jax.ShapeDtypeStruct((slots, ff), BF16),
            jax.ShapeDtypeStruct((slots, latent), BF16),
            jax.ShapeDtypeStruct((slots, latent), BF16),
            jax.ShapeDtypeStruct((slots, wide), BF16),
            jax.ShapeDtypeStruct((groups, slots, lw), BF16),
            jax.ShapeDtypeStruct((groups, slots, width), BF16),
            jax.ShapeDtypeStruct((lw, width), F32),
        ),
        in_specs=[hbm] * len(ins),
        out_specs=[vmem] * 9,
        scratch_shapes=[pltpu.VMEM(a.shape, a.dtype) for a in ins]
        + [
            pltpu.VMEM((groups, pad, width), BF16),
            pltpu.VMEM((groups, pad, width), BF16),
            pltpu.VMEM((groups, pad, wide), BF16),
            pltpu.VMEM((groups, pad, wide), BF16),
            pltpu.VMEM((groups, pad, width), BF16),
            pltpu.VMEM((groups - 1, lw, width), BF16),
            pltpu.VMEM((groups - 1, lw, width), BF16),
            pltpu.VMEM((slots, latent), F32),
            pltpu.VMEM((slots, latent), BF16),
            pltpu.VMEM((shares, block, latent), BF16),
            pltpu.VMEM((slots, wide), F32),
            pltpu.VMEM((slots, wide), BF16),
            pltpu.VMEM((shares, block, wide), BF16),
            pltpu.VMEM((slots, wide), BF16),
            pltpu.SemaphoreType.DMA((len(ins),)),
            pltpu.SemaphoreType.DMA((6, 2, groups)),
            pltpu.SemaphoreType.DMA((4, 2, shares)),
        ],
        compiler_params=pltpu.CompilerParams(
            collective_id=0, has_side_effects=True, vmem_limit_bytes=60 * 1024 * 1024
        ),
    )(*ins)
    outs = (
        jax.ShapeDtypeStruct((tokens, width), BF16),
        jax.ShapeDtypeStruct((lw, width), F32),
        jax.ShapeDtypeStruct((lw, width), F32),
        jax.ShapeDtypeStruct(ids_t.shape, F32),
        jax.ShapeDtypeStruct((ff, latent), F32),
        jax.ShapeDtypeStruct((ff, latent), F32),
    )
    input_grad, down_grad, up_grad, gate_grad, in_grad, out_grad = pl.pallas_call(
        functools.partial(outputs_kernel, groups, pad),
        out_shape=outs,
        in_specs=[vmem] * 11,
        out_specs=[hbm] * 6,
        scratch_shapes=[
            pltpu.VMEM(outs[n].shape, outs[n].dtype) for n in (0, 1, 3, 4, 5)
        ]
        + [pltpu.SemaphoreType.DMA((6,))],
        compiler_params=pltpu.CompilerParams(vmem_limit_bytes=56 * 1024 * 1024),
    )(*between, ids_t, down_proj)
    return (input_grad, down_grad, up_grad, gate_grad.T, in_grad.T[None], out_grad[None])


def padded_rows(tokens):
    return -(-(tokens * 3 // 32) // ROWS) * ROWS


def fits(layer_input, latent_saved, expert_in):
    groups = lax.axis_size("expert")
    shares = lax.axis_size("hidden")
    slots = groups * padded_rows(layer_input.shape[0])
    return (
        expert_in.shape[0] == 1
        and slots % (ROWS * shares) == 0
        and slots % LANES == 0
        and latent_saved.shape[1] % (LANES * groups) == 0
        and layer_input.shape[1] % LANES == 0
    )


def per_device(*arrays):
    run = fused if fits(arrays[0], arrays[2], arrays[8]) else on_device
    return run(*arrays)


def slot_layout(table, groups, local_count):
    tokens_here = table.shape[0]
    return table.T.reshape(groups, local_count, tokens_here).transpose(1, 0, 2)[:, :, None, :]


def on_device(
    layer_input,
    output_grad,
    latent_saved,
    combined_saved,
    expert_ids,
    gate_values,
    down_proj,
    up_proj,
    expert_in,
    expert_out,
):
    groups = lax.axis_size("expert")
    shares = lax.axis_size("hidden")
    tokens_here = layer_input.shape[0]
    latent_width = latent_saved.shape[1]
    local_count = expert_in.shape[0]
    capacity = tokens_here * 3 // 32
    live_count = local_count * groups
    slot_total = local_count * groups * capacity
    part_width = latent_width // shares
    partial_cot = jnp.einsum("td,ld->tl", output_grad, up_proj, preferred_element_type=jnp.float32)
    member = expert_ids[:, :, None] == jnp.arange(live_count, dtype=jnp.int32)[None, None, :]
    per_token = jnp.sum(member.astype(jnp.int32), axis=1)
    token_iota = jnp.arange(tokens_here, dtype=jnp.int32)
    earlier = (token_iota[None, :] < token_iota[:, None]).astype(jnp.bfloat16)
    before = jnp.dot(
        earlier, per_token.astype(jnp.bfloat16), preferred_element_type=jnp.float32
    ).astype(jnp.int32)
    gate_token = jnp.sum(
        jnp.where(member, gate_values.astype(jnp.float32)[:, :, None], 0.0), axis=1
    )
    rank_iota = jnp.arange(capacity, dtype=jnp.int32)[None, None, :, None]
    hit_slot = (slot_layout(per_token, groups, local_count) == 1) & (
        slot_layout(before, groups, local_count) == rank_iota
    )
    gate_slot = jnp.sum(
        jnp.where(hit_slot, slot_layout(gate_token, groups, local_count), 0.0), axis=3
    )
    gate_send = gate_slot.astype(jnp.bfloat16)
    dispatch_bf = hit_slot.astype(jnp.bfloat16).reshape(slot_total, tokens_here)
    cot_part = lax.psum_scatter(partial_cot, "hidden", scatter_dimension=1, tiled=True).astype(
        jnp.bfloat16
    )
    latent_part = lax.dynamic_slice_in_dim(
        latent_saved, lax.axis_index("hidden") * part_width, part_width, 1
    )
    cot_rows = jnp.dot(dispatch_bf, cot_part, preferred_element_type=jnp.float32).astype(
        jnp.bfloat16
    )
    latent_rows = jnp.dot(dispatch_bf, latent_part, preferred_element_type=jnp.float32).astype(
        jnp.bfloat16
    )
    cot_piece, latent_piece, gate_recv = (
        lax.all_to_all(
            cot_rows.reshape(local_count, groups, capacity, part_width),
            "expert",
            split_axis=1,
            concat_axis=1,
            tiled=True,
        ),
        lax.all_to_all(
            latent_rows.reshape(local_count, groups, capacity, part_width),
            "expert",
            split_axis=1,
            concat_axis=1,
            tiled=True,
        ),
        lax.all_to_all(gate_send, "expert", split_axis=1, concat_axis=1, tiled=True),
    )
    cot_recv, latent_recv = (
        lax.all_gather(cot_piece, "hidden", axis=3, tiled=True),
        lax.all_gather(latent_piece, "hidden", axis=3, tiled=True),
    )
    row_count = groups * capacity
    cot_block = cot_recv.reshape(local_count, row_count, latent_width)
    latent_block = latent_recv.reshape(local_count, row_count, latent_width)
    gate_block = gate_recv.reshape(local_count, row_count).astype(jnp.float32)
    pre_act = jnp.einsum(
        "erl,elf->erf", latent_block, expert_in, preferred_element_type=jnp.float32
    )
    relu_out = jnp.maximum(pre_act, 0.0)
    back_proj = jnp.einsum(
        "erl,efl->erf", cot_block, expert_out, preferred_element_type=jnp.float32
    )
    gate_part = jnp.sum(back_proj * relu_out * relu_out, axis=2)
    scaled_act = (gate_block[:, :, None] * relu_out * relu_out).astype(jnp.bfloat16)
    pre_grad = (2.0 * gate_block[:, :, None] * relu_out * back_proj).astype(jnp.bfloat16)
    expert_out_grad = jnp.einsum(
        "erf,erl->efl", scaled_act, cot_block, preferred_element_type=jnp.float32
    )
    expert_in_grad = jnp.einsum(
        "erl,erf->elf", latent_block, pre_grad, preferred_element_type=jnp.float32
    )
    latent_back = jnp.einsum(
        "erf,elf->erl", pre_grad, expert_in, preferred_element_type=jnp.float32
    )
    latent_back = latent_back.reshape(local_count, groups, capacity, latent_width)
    gate_part = gate_part.reshape(local_count, groups, capacity)
    dispatch_full = hit_slot.astype(jnp.float32)
    dispatch_flat = dispatch_full.reshape(slot_total, tokens_here)
    rows_home, gate_home = (
        lax.all_to_all(latent_back, "expert", split_axis=1, concat_axis=1, tiled=True),
        lax.all_to_all(gate_part, "expert", split_axis=1, concat_axis=1, tiled=True),
    )
    token_sums = jnp.dot(
        dispatch_flat.T,
        rows_home.reshape(slot_total, latent_width),
        precision=lax.Precision.HIGHEST,
        preferred_element_type=jnp.float32,
    )
    by_expert = jnp.sum(dispatch_full * gate_home[:, :, :, None], axis=2)
    by_expert = by_expert.transpose(2, 1, 0).reshape(tokens_here, live_count)
    gate_local = jnp.sum(jnp.where(member, by_expert[:, None, :], 0.0), axis=2)
    latent_grad, gate_grad = lax.psum((token_sums, gate_local), "hidden")
    latent_bf = latent_grad.astype(jnp.bfloat16)
    input_grad = jnp.dot(latent_bf, down_proj, preferred_element_type=jnp.float32).astype(
        jnp.bfloat16
    )
    down_term = jnp.einsum("tl,td->ld", latent_bf, layer_input, preferred_element_type=jnp.float32)
    up_term = jnp.einsum(
        "tl,td->ld", combined_saved, output_grad, preferred_element_type=jnp.float32
    )
    down_grad, up_grad = (
        lax.psum_scatter(down_term, "expert", scatter_dimension=0, tiled=True),
        lax.psum_scatter(up_term, "expert", scatter_dimension=0, tiled=True),
    )
    return (input_grad, down_grad, up_grad, gate_grad, expert_in_grad, expert_out_grad)


def solution(mesh):
    return jax.shard_map(
        per_device,
        mesh=mesh,
        in_specs=(
            P("expert", "hidden"),
            P("expert", "hidden"),
            P("expert", None),
            P("expert", None),
            P("expert", None),
            P("expert", None),
            P(None, "hidden"),
            P(None, "hidden"),
            P("expert", None, "hidden"),
            P("expert", "hidden", None),
        ),
        out_specs=(
            P("expert", "hidden"),
            P("expert", "hidden"),
            P("expert", "hidden"),
            P("expert", None),
            P("expert", None, "hidden"),
            P("expert", "hidden", None),
        ),
        check_vma=False,
    )
```

```python
import functools

import jax
import jax.numpy as jnp
from jax import lax
from jax.experimental import pallas as pl
from jax.experimental.pallas import tpu as pltpu
from jax.sharding import PartitionSpec as P

F32 = jnp.float32
BF16 = jnp.bfloat16
LANES = 128
ROWS = 16


def mm(a, b, ca, cb):
    return lax.dot_general(a, b, (((ca,), (cb,)), ((), ())), preferred_element_type=F32)


def rows_at(index, size):
    return pl.ds(pl.multiple_of(index * size, size), size)


def fused_kernel(
    groups,
    shares,
    pad,
    x_hbm,
    og_hbm,
    z_hbm,
    u_hbm,
    ids_hbm,
    gates_hbm,
    up_hbm,
    ein_hbm,
    eout_hbm,
    disp_ref,
    scaled_ref,
    pre_ref,
    zb_ref,
    cag,
    home,
    dn,
    x_r,
    ug_ref,
    x_ref,
    og_ref,
    z_ref,
    u_ref,
    ids_ref,
    gates_ref,
    up_ref,
    ein_ref,
    eout_ref,
    og_s,
    og_r,
    z_s,
    z_r,
    x_s,
    up_s,
    up_r,
    cf,
    ch,
    cs,
    cr,
    bf,
    bh,
    bs,
    br,
    bag,
    sems_in,
    sems_e,
    sems_h,
):
    e = lax.axis_index("expert")
    h = lax.axis_index("hidden")
    tokens = ids_ref.shape[1]
    slots = groups * pad
    latent = z_ref.shape[1]
    block = slots // shares
    lw = latent // groups

    def expert_peer(j):
        return lax.rem(e + j, groups)

    pairs = shares // 2
    core = lax.rem(h, 2)
    line = h // 2
    sibling = line * 2 + 1 - core

    def line_peer(j):
        return lax.rem(line + j, pairs)

    def line_source(j):
        return lax.rem(line + (pairs - j), pairs)

    def to_expert(phase, j, src, dst):
        copy = pltpu.make_async_remote_copy(
            src_ref=src,
            dst_ref=dst,
            send_sem=sems_e.at[phase, 0, j],
            recv_sem=sems_e.at[phase, 1, j],
            device_id=(expert_peer(j), h),
            device_id_type=pl.DeviceIdType.MESH,
        )
        copy.start()
        return copy

    def to_hidden(phase, j, peer, src, dst):
        copy = pltpu.make_async_remote_copy(
            src_ref=src,
            dst_ref=dst,
            send_sem=sems_h.at[phase, 0, j],
            recv_sem=sems_h.at[phase, 1, j],
            device_id=(e, peer),
            device_id_type=pl.DeviceIdType.MESH,
        )
        copy.start()
        return copy

    def swap_halves(phase, full, half):
        return to_hidden(phase, 0, sibling, full.at[:, 1 - core], half)

    def scatter_start(phase, swap, full, half, sends, lands):
        swap.wait_recv()
        sends[...] = (full[:, core] + half[...]).astype(BF16)
        return [
            to_hidden(
                phase, j, line_peer(j) * 2 + core, sends.at[line_peer(j)], lands.at[line]
            )
            for j in range(1, pairs)
        ]

    def scatter_sums(copies, full, half, lands):
        total = full[line, core] + half[line]
        for j in range(1, pairs):
            copies[j - 1].wait_recv()
            total = total + lands[line_source(j)].astype(F32)
        return total.astype(BF16)

    def gather_blocks(phase, full):
        mine = full.at[rows_at(h, block)]
        copies = [
            to_hidden(phase, j, line_peer(j) * 2 + core, mine, mine)
            for j in range(1, pairs)
        ]
        shared = [to_hidden(phase + 1, 0, sibling, mine, mine)]
        for j in range(1, pairs):
            copies[j - 1].wait_recv()
            theirs = full.at[rows_at(line_source(j) * 2 + core, block)]
            shared.append(to_hidden(phase + 1, j, sibling, theirs, theirs))
        return copies, shared

    sources = (ids_hbm, gates_hbm, og_hbm, z_hbm, up_hbm, ein_hbm, x_hbm, u_hbm, eout_hbm)
    targets = (ids_ref, gates_ref, og_ref, z_ref, up_ref, ein_ref, x_ref, u_ref, eout_ref)
    loads = [
        pltpu.make_async_copy(src, dst, sems_in.at[n])
        for n, (src, dst) in enumerate(zip(sources, targets))
    ]
    for load in loads:
        load.start()
    ids_in, gates_in, og_in, z_in, up_in, ein_in, x_in, u_in, eout_in = loads

    barrier = pltpu.get_barrier_semaphore()
    for j in range(1, groups):
        pl.semaphore_signal(
            barrier,
            inc=1,
            device_id=(expert_peer(j), h),
            device_id_type=pl.DeviceIdType.MESH,
        )
    for peer in [sibling] + [line_peer(j) * 2 + core for j in range(1, pairs)]:
        pl.semaphore_signal(
            barrier,
            inc=1,
            device_id=(e, peer),
            device_id_type=pl.DeviceIdType.MESH,
        )

    row_t = lax.broadcasted_iota(jnp.int32, (tokens, tokens), 0)
    col_t = lax.broadcasted_iota(jnp.int32, (tokens, tokens), 1)
    earlier = jnp.where(row_t < col_t, 1.0, 0.0).astype(BF16)
    ids_in.wait()
    gates_in.wait()
    ids = ids_ref[...]
    gates = gates_ref[...].astype(F32)
    member_rows = []
    gate_rows = []
    for n in range(groups):
        hit = ids == n
        member_rows.append(jnp.sum(jnp.where(hit, 1.0, 0.0), axis=0, keepdims=True))
        gate_rows.append(jnp.sum(jnp.where(hit, gates, 0.0), axis=0, keepdims=True))
    member = jnp.concatenate(
        [jnp.broadcast_to(row, (pad, tokens)) for row in member_rows], axis=0
    )
    gate_token = jnp.concatenate(
        [jnp.broadcast_to(row, (pad, tokens)) for row in gate_rows], axis=0
    )
    before = mm(member.astype(BF16), earlier, 1, 0)
    slot = lax.broadcasted_iota(jnp.int32, (slots, tokens), 0)
    rank = lax.rem(slot, pad).astype(F32)
    chosen = jnp.where(before == rank, member, 0.0)
    disp = chosen.astype(BF16)
    disp_ref[...] = disp
    og_in.wait()

    og_s[...] = mm(disp, og_ref[...], 1, 0).astype(BF16).reshape(og_s.shape)
    pl.semaphore_wait(barrier, groups + pairs - 1)
    og_c = [
        to_expert(0, j, og_s.at[expert_peer(j)], og_r.at[e]) for j in range(1, groups)
    ]
    z_in.wait()
    z_s[:, :, 0:latent] = mm(disp, z_ref[...], 1, 0).astype(BF16).reshape(groups, pad, latent)
    gate_col = jnp.sum(chosen * gate_token, axis=1, keepdims=True)
    z_s[:, :, latent : latent + LANES] = (
        jnp.broadcast_to(gate_col, (slots, LANES)).astype(BF16).reshape(groups, pad, LANES)
    )
    z_c = [to_expert(1, j, z_s.at[expert_peer(j)], z_r.at[e]) for j in range(1, groups)]
    og_r[e] = og_s[e]
    z_r[e] = z_s[e]
    x_in.wait()
    x_s[...] = mm(disp, x_ref[...], 1, 0).astype(BF16).reshape(x_s.shape)
    x_r[:, rows_at(e, pad), :] = x_s[...]
    u_in.wait()
    for j in range(1, groups):
        up_s[j - 1] = mm(
            u_ref[:, rows_at(expert_peer(j), lw)], og_ref[...], 0, 0
        ).astype(BF16)
    ug_ref[...] = mm(u_ref[:, rows_at(e, lw)], og_ref[...], 0, 0)

    for c in og_c:
        c.wait_recv()
    up_in.wait()
    cot_part = mm(og_r[...].reshape(slots, og_ref.shape[1]), up_ref[...], 1, 1)
    cf[...] = cot_part.reshape(cf.shape)
    cot_swap = swap_halves(0, cf, ch)
    crs = scatter_start(1, cot_swap, cf, ch, cs, cr)
    for c in z_c:
        c.wait_recv()
    x_c = [
        to_expert(2, j, x_s, x_r.at[:, rows_at(e, pad), :]) for j in range(1, groups)
    ]
    up_c = [to_expert(3, j, up_s.at[j - 1], up_r.at[j - 1]) for j in range(1, groups)]
    zb = z_r[:, :, 0:latent].reshape(slots, latent)
    gate_b = z_r[:, :, latent : latent + LANES].astype(F32).reshape(slots, LANES)[:, 0:1]
    zb_ref[...] = zb
    ein_in.wait()
    act = jnp.maximum(mm(zb, ein_ref[...], 1, 1), 0.0)
    square = act * act
    scaled_ref[...] = (gate_b * square).astype(BF16)
    eout_in.wait()
    cag[rows_at(h, block), :] = scatter_sums(crs, cf, ch, cr)
    cagc, cags = gather_blocks(2, cag)
    for c in cags:
        c.wait_recv()

    cotb = cag[...]
    back = mm(cotb, eout_ref[...], 1, 1)
    gate_part = jnp.sum(back * square, axis=1, keepdims=True)
    pre_grad = ((2.0 * gate_b) * act * back).astype(BF16)
    pre_ref[...] = pre_grad
    part = mm(pre_grad, ein_ref[...], 1, 0)
    gate_wide = jnp.broadcast_to(gate_part, (slots, LANES))
    bf[:, :, :, 0:latent] = part.reshape(pairs, 2, block, latent)
    bf[:, :, :, latent : latent + LANES] = gate_wide.reshape(pairs, 2, block, LANES)
    back_swap = swap_halves(4, bf, bh)
    brs = scatter_start(5, back_swap, bf, bh, bs, br)
    bag[rows_at(h, block), :] = scatter_sums(brs, bf, bh, br)
    bagc, bags = gather_blocks(6, bag)
    for j in range(1, groups):
        up_c[j - 1].wait_recv()
        ug_ref[...] += up_r[j - 1].astype(F32)
    for c in x_c:
        c.wait_recv()
    for c in bags:
        c.wait_recv()

    home_c = [
        to_expert(4, j, bag.at[rows_at(expert_peer(j), pad)], home.at[rows_at(e, pad)])
        for j in range(1, groups)
    ]
    dn_c = [
        to_expert(5, j, bag.at[:, rows_at(expert_peer(j), lw)], dn.at[e])
        for j in range(1, groups)
    ]
    home[rows_at(e, pad), :] = bag[rows_at(e, pad), :]
    dn[e] = bag[:, rows_at(e, lw)]
    for c in home_c + dn_c:
        c.wait_recv()
    sent = og_c + z_c + [cot_swap] + crs + x_c + up_c + cagc + cags
    sent += [back_swap] + brs + bagc + bags + home_c + dn_c
    for c in sent:
        c.wait_send()


def outputs_kernel(
    groups,
    pad,
    disp_ref,
    scaled_ref,
    pre_ref,
    zb_ref,
    cot_ref,
    home_ref,
    dn_ref,
    x_ref,
    ug_ref,
    ids_ref,
    down_ref,
    ig_hbm,
    dg_hbm,
    ug_hbm,
    gg_hbm,
    eig_hbm,
    eog_hbm,
    ig_v,
    dg_v,
    gg_v,
    eig_v,
    eog_v,
    sems,
):
    slots = groups * pad
    latent = cot_ref.shape[1]
    stores = []

    def store(src, dst):
        copy = pltpu.make_async_copy(src, dst, sems.at[len(stores)])
        copy.start()
        stores.append(copy)

    store(ug_ref, ug_hbm)
    eog_v[...] = mm(scaled_ref[...], cot_ref[...], 0, 0)
    store(eog_v, eog_hbm)
    eig_v[...] = mm(pre_ref[...], zb_ref[...], 0, 0)
    store(eig_v, eig_hbm)
    dg_v[...] = mm(
        dn_ref[...].reshape(groups * slots, dn_ref.shape[2]),
        x_ref[...].reshape(groups * slots, x_ref.shape[2]),
        0,
        0,
    )
    store(dg_v, dg_hbm)
    disp = disp_ref[...]
    latent_grad = mm(disp, home_ref[:, 0:latent], 0, 0).astype(BF16)
    ig_v[...] = mm(latent_grad, down_ref[...], 1, 0).astype(BF16)
    store(ig_v, ig_hbm)
    by_slot = home_ref[:, latent : latent + LANES].astype(F32)[:, 0:1] * disp.astype(F32)
    ids = ids_ref[...]
    gate_out = jnp.zeros(ids.shape, F32)
    for n in range(groups):
        by_token = jnp.sum(by_slot[n * pad : (n + 1) * pad], axis=0, keepdims=True)
        gate_out = jnp.where(ids == n, by_token, gate_out)
    gg_v[...] = gate_out
    store(gg_v, gg_hbm)
    for copy in stores:
        copy.wait()


def fused(
    layer_input,
    output_grad,
    latent_saved,
    combined_saved,
    expert_ids,
    gate_values,
    down_proj,
    up_proj,
    expert_in,
    expert_out,
):
    groups = lax.axis_size("expert")
    shares = lax.axis_size("hidden")
    tokens, width = layer_input.shape
    latent = latent_saved.shape[1]
    ff = expert_in.shape[2]
    pad = padded_rows(tokens)
    slots = groups * pad
    block = slots // shares
    wide = latent + LANES
    lw = latent // groups
    vmem = pl.BlockSpec(memory_space=pltpu.VMEM)
    hbm = pl.BlockSpec(memory_space=pltpu.HBM)
    ids_t = expert_ids.T
    ins = (
        layer_input,
        output_grad,
        latent_saved,
        combined_saved,
        ids_t,
        gate_values.T,
        up_proj,
        expert_in[0].T,
        expert_out[0],
    )
    between = pl.pallas_call(
        functools.partial(fused_kernel, groups, shares, pad),
        out_shape=(
            jax.ShapeDtypeStruct((slots, tokens), BF16),
            jax.ShapeDtypeStruct((slots, ff), BF16),
            jax.ShapeDtypeStruct((slots, ff), BF16),
            jax.ShapeDtypeStruct((slots, latent), BF16),
            jax.ShapeDtypeStruct((slots, latent), BF16),
            jax.ShapeDtypeStruct((slots, wide), BF16),
            jax.ShapeDtypeStruct((groups, slots, lw), BF16),
            jax.ShapeDtypeStruct((groups, slots, width), BF16),
            jax.ShapeDtypeStruct((lw, width), F32),
        ),
        in_specs=[hbm] * len(ins),
        out_specs=[vmem] * 9,
        scratch_shapes=[pltpu.VMEM(a.shape, a.dtype) for a in ins]
        + [
            pltpu.VMEM((groups, pad, width), BF16),
            pltpu.VMEM((groups, pad, width), BF16),
            pltpu.VMEM((groups, pad, wide), BF16),
            pltpu.VMEM((groups, pad, wide), BF16),
            pltpu.VMEM((groups, pad, width), BF16),
            pltpu.VMEM((groups - 1, lw, width), BF16),
            pltpu.VMEM((groups - 1, lw, width), BF16),
            pltpu.VMEM((shares // 2, 2, block, latent), F32),
            pltpu.VMEM((shares // 2, block, latent), F32),
            pltpu.VMEM((shares // 2, block, latent), BF16),
            pltpu.VMEM((shares // 2, block, latent), BF16),
            pltpu.VMEM((shares // 2, 2, block, wide), F32),
            pltpu.VMEM((shares // 2, block, wide), F32),
            pltpu.VMEM((shares // 2, block, wide), BF16),
            pltpu.VMEM((shares // 2, block, wide), BF16),
            pltpu.VMEM((slots, wide), BF16),
            pltpu.SemaphoreType.DMA((len(ins),)),
            pltpu.SemaphoreType.DMA((6, 2, groups)),
            pltpu.SemaphoreType.DMA((8, 2, shares // 2)),
        ],
        compiler_params=pltpu.CompilerParams(
            collective_id=0, has_side_effects=True, vmem_limit_bytes=60 * 1024 * 1024
        ),
    )(*ins)
    outs = (
        jax.ShapeDtypeStruct((tokens, width), BF16),
        jax.ShapeDtypeStruct((lw, width), F32),
        jax.ShapeDtypeStruct((lw, width), F32),
        jax.ShapeDtypeStruct(ids_t.shape, F32),
        jax.ShapeDtypeStruct((ff, latent), F32),
        jax.ShapeDtypeStruct((ff, latent), F32),
    )
    input_grad, down_grad, up_grad, gate_grad, in_grad, out_grad = pl.pallas_call(
        functools.partial(outputs_kernel, groups, pad),
        out_shape=outs,
        in_specs=[vmem] * 11,
        out_specs=[hbm] * 6,
        scratch_shapes=[
            pltpu.VMEM(outs[n].shape, outs[n].dtype) for n in (0, 1, 3, 4, 5)
        ]
        + [pltpu.SemaphoreType.DMA((6,))],
        compiler_params=pltpu.CompilerParams(vmem_limit_bytes=56 * 1024 * 1024),
    )(*between, ids_t, down_proj)
    return (input_grad, down_grad, up_grad, gate_grad.T, in_grad.T[None], out_grad[None])


def padded_rows(tokens):
    return -(-(tokens * 3 // 32) // ROWS) * ROWS


def fits(layer_input, latent_saved, expert_in):
    groups = lax.axis_size("expert")
    shares = lax.axis_size("hidden")
    slots = groups * padded_rows(layer_input.shape[0])
    return (
        expert_in.shape[0] == 1
        and shares % 2 == 0
        and slots % (ROWS * shares) == 0
        and slots % LANES == 0
        and latent_saved.shape[1] % (LANES * groups) == 0
        and layer_input.shape[1] % LANES == 0
    )


def per_device(*arrays):
    run = fused if fits(arrays[0], arrays[2], arrays[8]) else on_device
    return run(*arrays)


def slot_layout(table, groups, local_count):
    tokens_here = table.shape[0]
    return table.T.reshape(groups, local_count, tokens_here).transpose(1, 0, 2)[:, :, None, :]


def on_device(
    layer_input,
    output_grad,
    latent_saved,
    combined_saved,
    expert_ids,
    gate_values,
    down_proj,
    up_proj,
    expert_in,
    expert_out,
):
    groups = lax.axis_size("expert")
    shares = lax.axis_size("hidden")
    tokens_here = layer_input.shape[0]
    latent_width = latent_saved.shape[1]
    local_count = expert_in.shape[0]
    capacity = tokens_here * 3 // 32
    live_count = local_count * groups
    slot_total = local_count * groups * capacity
    part_width = latent_width // shares
    partial_cot = jnp.einsum("td,ld->tl", output_grad, up_proj, preferred_element_type=jnp.float32)
    member = expert_ids[:, :, None] == jnp.arange(live_count, dtype=jnp.int32)[None, None, :]
    per_token = jnp.sum(member.astype(jnp.int32), axis=1)
    token_iota = jnp.arange(tokens_here, dtype=jnp.int32)
    earlier = (token_iota[None, :] < token_iota[:, None]).astype(jnp.bfloat16)
    before = jnp.dot(
        earlier, per_token.astype(jnp.bfloat16), preferred_element_type=jnp.float32
    ).astype(jnp.int32)
    gate_token = jnp.sum(
        jnp.where(member, gate_values.astype(jnp.float32)[:, :, None], 0.0), axis=1
    )
    rank_iota = jnp.arange(capacity, dtype=jnp.int32)[None, None, :, None]
    hit_slot = (slot_layout(per_token, groups, local_count) == 1) & (
        slot_layout(before, groups, local_count) == rank_iota
    )
    gate_slot = jnp.sum(
        jnp.where(hit_slot, slot_layout(gate_token, groups, local_count), 0.0), axis=3
    )
    gate_send = gate_slot.astype(jnp.bfloat16)
    dispatch_bf = hit_slot.astype(jnp.bfloat16).reshape(slot_total, tokens_here)
    cot_part = lax.psum_scatter(partial_cot, "hidden", scatter_dimension=1, tiled=True).astype(
        jnp.bfloat16
    )
    latent_part = lax.dynamic_slice_in_dim(
        latent_saved, lax.axis_index("hidden") * part_width, part_width, 1
    )
    cot_rows = jnp.dot(dispatch_bf, cot_part, preferred_element_type=jnp.float32).astype(
        jnp.bfloat16
    )
    latent_rows = jnp.dot(dispatch_bf, latent_part, preferred_element_type=jnp.float32).astype(
        jnp.bfloat16
    )
    cot_piece, latent_piece, gate_recv = (
        lax.all_to_all(
            cot_rows.reshape(local_count, groups, capacity, part_width),
            "expert",
            split_axis=1,
            concat_axis=1,
            tiled=True,
        ),
        lax.all_to_all(
            latent_rows.reshape(local_count, groups, capacity, part_width),
            "expert",
            split_axis=1,
            concat_axis=1,
            tiled=True,
        ),
        lax.all_to_all(gate_send, "expert", split_axis=1, concat_axis=1, tiled=True),
    )
    cot_recv, latent_recv = (
        lax.all_gather(cot_piece, "hidden", axis=3, tiled=True),
        lax.all_gather(latent_piece, "hidden", axis=3, tiled=True),
    )
    row_count = groups * capacity
    cot_block = cot_recv.reshape(local_count, row_count, latent_width)
    latent_block = latent_recv.reshape(local_count, row_count, latent_width)
    gate_block = gate_recv.reshape(local_count, row_count).astype(jnp.float32)
    pre_act = jnp.einsum(
        "erl,elf->erf", latent_block, expert_in, preferred_element_type=jnp.float32
    )
    relu_out = jnp.maximum(pre_act, 0.0)
    back_proj = jnp.einsum(
        "erl,efl->erf", cot_block, expert_out, preferred_element_type=jnp.float32
    )
    gate_part = jnp.sum(back_proj * relu_out * relu_out, axis=2)
    scaled_act = (gate_block[:, :, None] * relu_out * relu_out).astype(jnp.bfloat16)
    pre_grad = (2.0 * gate_block[:, :, None] * relu_out * back_proj).astype(jnp.bfloat16)
    expert_out_grad = jnp.einsum(
        "erf,erl->efl", scaled_act, cot_block, preferred_element_type=jnp.float32
    )
    expert_in_grad = jnp.einsum(
        "erl,erf->elf", latent_block, pre_grad, preferred_element_type=jnp.float32
    )
    latent_back = jnp.einsum(
        "erf,elf->erl", pre_grad, expert_in, preferred_element_type=jnp.float32
    )
    latent_back = latent_back.reshape(local_count, groups, capacity, latent_width)
    gate_part = gate_part.reshape(local_count, groups, capacity)
    dispatch_full = hit_slot.astype(jnp.float32)
    dispatch_flat = dispatch_full.reshape(slot_total, tokens_here)
    rows_home, gate_home = (
        lax.all_to_all(latent_back, "expert", split_axis=1, concat_axis=1, tiled=True),
        lax.all_to_all(gate_part, "expert", split_axis=1, concat_axis=1, tiled=True),
    )
    token_sums = jnp.dot(
        dispatch_flat.T,
        rows_home.reshape(slot_total, latent_width),
        precision=lax.Precision.HIGHEST,
        preferred_element_type=jnp.float32,
    )
    by_expert = jnp.sum(dispatch_full * gate_home[:, :, :, None], axis=2)
    by_expert = by_expert.transpose(2, 1, 0).reshape(tokens_here, live_count)
    gate_local = jnp.sum(jnp.where(member, by_expert[:, None, :], 0.0), axis=2)
    latent_grad, gate_grad = lax.psum((token_sums, gate_local), "hidden")
    latent_bf = latent_grad.astype(jnp.bfloat16)
    input_grad = jnp.dot(latent_bf, down_proj, preferred_element_type=jnp.float32).astype(
        jnp.bfloat16
    )
    down_term = jnp.einsum("tl,td->ld", latent_bf, layer_input, preferred_element_type=jnp.float32)
    up_term = jnp.einsum(
        "tl,td->ld", combined_saved, output_grad, preferred_element_type=jnp.float32
    )
    down_grad, up_grad = (
        lax.psum_scatter(down_term, "expert", scatter_dimension=0, tiled=True),
        lax.psum_scatter(up_term, "expert", scatter_dimension=0, tiled=True),
    )
    return (input_grad, down_grad, up_grad, gate_grad, expert_in_grad, expert_out_grad)


def solution(mesh):
    return jax.shard_map(
        per_device,
        mesh=mesh,
        in_specs=(
            P("expert", "hidden"),
            P("expert", "hidden"),
            P("expert", None),
            P("expert", None),
            P("expert", None),
            P("expert", None),
            P(None, "hidden"),
            P(None, "hidden"),
            P("expert", None, "hidden"),
            P("expert", "hidden", None),
        ),
        out_specs=(
            P("expert", "hidden"),
            P("expert", "hidden"),
            P("expert", "hidden"),
            P("expert", None),
            P("expert", None, "hidden"),
            P("expert", "hidden", None),
        ),
        check_vma=False,
    )
```

```python
import functools

import jax
import jax.numpy as jnp
from jax import lax
from jax.experimental import pallas as pl
from jax.experimental.pallas import tpu as pltpu
from jax.sharding import PartitionSpec as P

F32 = jnp.float32
BF16 = jnp.bfloat16
LANES = 128
ROWS = 16


def mm(a, b, ca, cb):
    return lax.dot_general(a, b, (((ca,), (cb,)), ((), ())), preferred_element_type=F32)


def rows_at(index, size):
    return pl.ds(pl.multiple_of(index * size, size), size)


def fused_kernel(
    groups,
    shares,
    pad,
    x_hbm,
    og_hbm,
    z_hbm,
    u_hbm,
    ids_hbm,
    gates_hbm,
    up_hbm,
    ein_hbm,
    eout_hbm,
    disp_ref,
    scaled_ref,
    pre_ref,
    zb_ref,
    cag,
    home,
    dn,
    x_r,
    ug_ref,
    x_ref,
    og_ref,
    z_ref,
    u_ref,
    ids_ref,
    gates_ref,
    up_ref,
    ein_ref,
    eout_ref,
    og_s,
    og_r,
    z_s,
    z_r,
    x_s,
    up_s,
    up_r,
    cf,
    ch,
    cs,
    cr,
    bf,
    bh,
    bs,
    br,
    bag,
    sems_in,
    sems_e,
    sems_h,
):
    e = lax.axis_index("expert")
    h = lax.axis_index("hidden")
    tokens = ids_ref.shape[1]
    slots = groups * pad
    latent = z_ref.shape[1]
    block = slots // shares
    lw = latent // groups

    def expert_peer(j):
        return lax.rem(e + j, groups)

    pairs = shares // 2
    core = lax.rem(h, 2)
    line = h // 2
    sibling = line * 2 + 1 - core

    def line_peer(j):
        return lax.rem(line + j, pairs)

    def line_source(j):
        return lax.rem(line + (pairs - j), pairs)

    def to_expert(phase, j, src, dst):
        copy = pltpu.make_async_remote_copy(
            src_ref=src,
            dst_ref=dst,
            send_sem=sems_e.at[phase, 0, j],
            recv_sem=sems_e.at[phase, 1, j],
            device_id=(expert_peer(j), h),
            device_id_type=pl.DeviceIdType.MESH,
        )
        copy.start()
        return copy

    def to_hidden(phase, j, peer, src, dst):
        copy = pltpu.make_async_remote_copy(
            src_ref=src,
            dst_ref=dst,
            send_sem=sems_h.at[phase, 0, j],
            recv_sem=sems_h.at[phase, 1, j],
            device_id=(e, peer),
            device_id_type=pl.DeviceIdType.MESH,
        )
        copy.start()
        return copy

    def to_sibling(phase, j, src, dst):
        copy = pltpu.make_async_remote_copy(
            src_ref=src,
            dst_ref=dst,
            send_sem=sems_e.at[phase, 0, j],
            recv_sem=sems_e.at[phase, 1, j],
            device_id=(e, sibling),
            device_id_type=pl.DeviceIdType.MESH,
        )
        copy.start()
        return copy

    def expert_source(j):
        return lax.rem(e + (groups - j), groups)

    def swap_halves(phase, full, half):
        return to_hidden(phase, 0, sibling, full.at[:, 1 - core], half)

    def scatter_start(phase, swap, full, half, sends, lands):
        swap.wait_recv()
        sends[...] = (full[:, core] + half[...]).astype(BF16)
        return [
            to_hidden(
                phase, j, line_peer(j) * 2 + core, sends.at[line_peer(j)], lands.at[line]
            )
            for j in range(1, pairs)
        ]

    def scatter_sums(copies, full, half, lands):
        total = full[line, core] + half[line]
        for j in range(1, pairs):
            copies[j - 1].wait_recv()
            total = total + lands[line_source(j)].astype(F32)
        return total.astype(BF16)

    def gather_blocks(phase, full):
        mine = full.at[rows_at(h, block)]
        copies = [
            to_hidden(phase, j, line_peer(j) * 2 + core, mine, mine)
            for j in range(1, pairs)
        ]
        shared = [to_hidden(phase + 1, 0, sibling, mine, mine)]
        for j in range(1, pairs):
            copies[j - 1].wait_recv()
            theirs = full.at[rows_at(line_source(j) * 2 + core, block)]
            shared.append(to_hidden(phase + 1, j, sibling, theirs, theirs))
        return copies, shared

    sources = (ids_hbm, gates_hbm, og_hbm, z_hbm, up_hbm, ein_hbm, x_hbm, u_hbm, eout_hbm)
    targets = (ids_ref, gates_ref, og_ref, z_ref, up_ref, ein_ref, x_ref, u_ref, eout_ref)
    loads = [
        pltpu.make_async_copy(src, dst, sems_in.at[n])
        for n, (src, dst) in enumerate(zip(sources, targets))
    ]
    for load in loads:
        load.start()
    ids_in, gates_in, og_in, z_in, up_in, ein_in, x_in, u_in, eout_in = loads

    barrier = pltpu.get_barrier_semaphore()
    for j in range(1, groups):
        pl.semaphore_signal(
            barrier,
            inc=1,
            device_id=(expert_peer(j), h),
            device_id_type=pl.DeviceIdType.MESH,
        )
    for peer in [sibling] + [line_peer(j) * 2 + core for j in range(1, pairs)]:
        pl.semaphore_signal(
            barrier,
            inc=1,
            device_id=(e, peer),
            device_id_type=pl.DeviceIdType.MESH,
        )

    row_t = lax.broadcasted_iota(jnp.int32, (tokens, tokens), 0)
    col_t = lax.broadcasted_iota(jnp.int32, (tokens, tokens), 1)
    earlier = jnp.where(row_t < col_t, 1.0, 0.0).astype(BF16)
    ids_in.wait()
    gates_in.wait()
    ids = ids_ref[...]
    gates = gates_ref[...].astype(F32)
    member_rows = []
    gate_rows = []
    for n in range(groups):
        hit = ids == n
        member_rows.append(jnp.sum(jnp.where(hit, 1.0, 0.0), axis=0, keepdims=True))
        gate_rows.append(jnp.sum(jnp.where(hit, gates, 0.0), axis=0, keepdims=True))
    member = jnp.concatenate(
        [jnp.broadcast_to(row, (pad, tokens)) for row in member_rows], axis=0
    )
    gate_token = jnp.concatenate(
        [jnp.broadcast_to(row, (pad, tokens)) for row in gate_rows], axis=0
    )
    before = mm(member.astype(BF16), earlier, 1, 0)
    slot = lax.broadcasted_iota(jnp.int32, (slots, tokens), 0)
    rank = lax.rem(slot, pad).astype(F32)
    chosen = jnp.where(before == rank, member, 0.0)
    disp = chosen.astype(BF16)
    disp_ref[...] = disp
    og_in.wait()

    og_s[...] = mm(disp, og_ref[...], 1, 0).astype(BF16).reshape(og_s.shape)
    pl.semaphore_wait(barrier, groups + pairs - 1)
    og_c = [
        to_expert(0, j, og_s.at[expert_peer(j)], og_r.at[e]) for j in range(1, groups)
    ]
    z_in.wait()
    z_s[:, :, 0:latent] = mm(disp, z_ref[...], 1, 0).astype(BF16).reshape(groups, pad, latent)
    gate_col = jnp.sum(chosen * gate_token, axis=1, keepdims=True)
    z_s[:, :, latent : latent + LANES] = (
        jnp.broadcast_to(gate_col, (slots, LANES)).astype(BF16).reshape(groups, pad, LANES)
    )
    my_rows = rows_at(core, pad // 2)
    z_c = [
        to_expert(1, j, z_s.at[expert_peer(j), my_rows], z_r.at[e, my_rows])
        for j in range(1, groups)
    ]
    og_r[e] = og_s[e]
    z_r[e] = z_s[e]
    x_in.wait()
    x_s[...] = mm(disp, x_ref[...], 1, 0).astype(BF16).reshape(x_s.shape)
    x_r[:, rows_at(e, pad), :] = x_s[...]
    u_in.wait()
    for j in range(1, groups):
        up_s[j - 1] = mm(
            u_ref[:, rows_at(expert_peer(j), lw)], og_ref[...], 0, 0
        ).astype(BF16)
    ug_ref[...] = mm(u_ref[:, rows_at(e, lw)], og_ref[...], 0, 0)

    for c in og_c:
        c.wait_recv()
    up_in.wait()
    cot_part = mm(og_r[...].reshape(slots, og_ref.shape[1]), up_ref[...], 1, 1)
    cf[...] = cot_part.reshape(cf.shape)
    cot_swap = swap_halves(0, cf, ch)
    crs = scatter_start(1, cot_swap, cf, ch, cs, cr)
    z_f = []
    for j in range(1, groups):
        z_c[j - 1].wait_recv()
        landed = z_r.at[expert_source(j), my_rows]
        z_f.append(to_sibling(6, j, landed, landed))
    x_c = [
        to_expert(2, j, x_s, x_r.at[:, rows_at(e, pad), :]) for j in range(1, groups)
    ]
    up_c = [to_expert(3, j, up_s.at[j - 1], up_r.at[j - 1]) for j in range(1, groups)]
    for c in z_f:
        c.wait_recv()
    zb = z_r[:, :, 0:latent].reshape(slots, latent)
    gate_b = z_r[:, :, latent : latent + LANES].astype(F32).reshape(slots, LANES)[:, 0:1]
    zb_ref[...] = zb
    ein_in.wait()
    act = jnp.maximum(mm(zb, ein_ref[...], 1, 1), 0.0)
    square = act * act
    scaled_ref[...] = (gate_b * square).astype(BF16)
    eout_in.wait()
    cag[rows_at(h, block), :] = scatter_sums(crs, cf, ch, cr)
    cagc, cags = gather_blocks(2, cag)
    for c in cags:
        c.wait_recv()

    cotb = cag[...]
    back = mm(cotb, eout_ref[...], 1, 1)
    gate_part = jnp.sum(back * square, axis=1, keepdims=True)
    pre_grad = ((2.0 * gate_b) * act * back).astype(BF16)
    pre_ref[...] = pre_grad
    part = mm(pre_grad, ein_ref[...], 1, 0)
    gate_wide = jnp.broadcast_to(gate_part, (slots, LANES))
    bf[:, :, :, 0:latent] = part.reshape(pairs, 2, block, latent)
    bf[:, :, :, latent : latent + LANES] = gate_wide.reshape(pairs, 2, block, LANES)
    back_swap = swap_halves(4, bf, bh)
    brs = scatter_start(5, back_swap, bf, bh, bs, br)
    bag[rows_at(h, block), :] = scatter_sums(brs, bf, bh, br)
    bagc, bags = gather_blocks(6, bag)
    for j in range(1, groups):
        up_c[j - 1].wait_recv()
        ug_ref[...] += up_r[j - 1].astype(F32)
    for c in x_c:
        c.wait_recv()
    for c in bags:
        c.wait_recv()

    half_pad = pad // 2
    my_half = rows_at(core, slots // 2)
    home_c = [
        to_expert(
            4,
            j,
            bag.at[rows_at(expert_peer(j) * 2 + core, half_pad)],
            home.at[rows_at(e * 2 + core, half_pad)],
        )
        for j in range(1, groups)
    ]
    dn_c = [
        to_expert(5, j, bag.at[my_half, rows_at(expert_peer(j), lw)], dn.at[e, my_half])
        for j in range(1, groups)
    ]
    home[rows_at(e, pad), :] = bag[rows_at(e, pad), :]
    dn[e] = bag[:, rows_at(e, lw)]
    last_f = []
    for j in range(1, groups):
        home_c[j - 1].wait_recv()
        landed = home.at[rows_at(expert_source(j) * 2 + core, half_pad)]
        last_f.append(to_sibling(7, j, landed, landed))
    for j in range(1, groups):
        dn_c[j - 1].wait_recv()
        landed = dn.at[expert_source(j), my_half]
        last_f.append(to_sibling(8, j, landed, landed))
    for c in last_f:
        c.wait_recv()
    sent = og_c + z_c + [cot_swap] + crs + x_c + up_c + cagc + cags
    sent += [back_swap] + brs + bagc + bags + home_c + dn_c + z_f + last_f
    for c in sent:
        c.wait_send()


def outputs_kernel(
    groups,
    pad,
    *refs,
):
    sources, refs = refs[:11], refs[11:]
    (ig_hbm, dg_hbm, ug_hbm, gg_hbm, eig_hbm, eog_hbm), refs = refs[:6], refs[6:]
    targets, refs = refs[:11], refs[11:]
    ig_v, dg_v, gg_v, eig_v, eog_v, sems, sems_in = refs
    (
        disp_ref,
        scaled_ref,
        pre_ref,
        zb_ref,
        cot_ref,
        home_ref,
        dn_ref,
        x_ref,
        ug_ref,
        ids_ref,
        down_ref,
    ) = targets
    loads = [
        pltpu.make_async_copy(src, dst, sems_in.at[n])
        for n, (src, dst) in enumerate(zip(sources, targets))
    ]
    order = (1, 4, 2, 3, 8, 6, 7, 0, 5, 10, 9)
    for n in order:
        loads[n].start()
    slots = groups * pad
    latent = cot_ref.shape[1]
    stores = []

    def store(src, dst):
        copy = pltpu.make_async_copy(src, dst, sems.at[len(stores)])
        copy.start()
        stores.append(copy)

    loads[1].wait()
    loads[4].wait()
    eog_v[...] = mm(scaled_ref[...], cot_ref[...], 0, 0)
    store(eog_v, eog_hbm)
    loads[2].wait()
    loads[3].wait()
    eig_v[...] = mm(pre_ref[...], zb_ref[...], 0, 0)
    store(eig_v, eig_hbm)
    loads[8].wait()
    store(ug_ref, ug_hbm)
    loads[6].wait()
    loads[7].wait()
    dg_v[...] = mm(
        dn_ref[...].reshape(groups * slots, dn_ref.shape[2]),
        x_ref[...].reshape(groups * slots, x_ref.shape[2]),
        0,
        0,
    )
    store(dg_v, dg_hbm)
    for n in (0, 5, 10, 9):
        loads[n].wait()
    disp = disp_ref[...]
    latent_grad = mm(disp, home_ref[:, 0:latent], 0, 0).astype(BF16)
    ig_v[...] = mm(latent_grad, down_ref[...], 1, 0).astype(BF16)
    store(ig_v, ig_hbm)
    by_slot = home_ref[:, latent : latent + LANES].astype(F32)[:, 0:1] * disp.astype(F32)
    ids = ids_ref[...]
    gate_out = jnp.zeros(ids.shape, F32)
    for n in range(groups):
        by_token = jnp.sum(by_slot[n * pad : (n + 1) * pad], axis=0, keepdims=True)
        gate_out = jnp.where(ids == n, by_token, gate_out)
    gg_v[...] = gate_out
    store(gg_v, gg_hbm)
    for copy in stores:
        copy.wait()


def fused(
    layer_input,
    output_grad,
    latent_saved,
    combined_saved,
    expert_ids,
    gate_values,
    down_proj,
    up_proj,
    expert_in,
    expert_out,
):
    groups = lax.axis_size("expert")
    shares = lax.axis_size("hidden")
    tokens, width = layer_input.shape
    latent = latent_saved.shape[1]
    ff = expert_in.shape[2]
    pad = padded_rows(tokens)
    slots = groups * pad
    block = slots // shares
    wide = latent + LANES
    lw = latent // groups
    vmem = pl.BlockSpec(memory_space=pltpu.VMEM)
    hbm = pl.BlockSpec(memory_space=pltpu.HBM)
    ids_t = expert_ids.T
    ins = (
        layer_input,
        output_grad,
        latent_saved,
        combined_saved,
        ids_t,
        gate_values.T,
        up_proj,
        expert_in[0].T,
        expert_out[0],
    )
    between = pl.pallas_call(
        functools.partial(fused_kernel, groups, shares, pad),
        out_shape=(
            jax.ShapeDtypeStruct((slots, tokens), BF16),
            jax.ShapeDtypeStruct((slots, ff), BF16),
            jax.ShapeDtypeStruct((slots, ff), BF16),
            jax.ShapeDtypeStruct((slots, latent), BF16),
            jax.ShapeDtypeStruct((slots, latent), BF16),
            jax.ShapeDtypeStruct((slots, wide), BF16),
            jax.ShapeDtypeStruct((groups, slots, lw), BF16),
            jax.ShapeDtypeStruct((groups, slots, width), BF16),
            jax.ShapeDtypeStruct((lw, width), F32),
        ),
        in_specs=[hbm] * len(ins),
        out_specs=[vmem] * 9,
        scratch_shapes=[pltpu.VMEM(a.shape, a.dtype) for a in ins]
        + [
            pltpu.VMEM((groups, pad, width), BF16),
            pltpu.VMEM((groups, pad, width), BF16),
            pltpu.VMEM((groups, pad, wide), BF16),
            pltpu.VMEM((groups, pad, wide), BF16),
            pltpu.VMEM((groups, pad, width), BF16),
            pltpu.VMEM((groups - 1, lw, width), BF16),
            pltpu.VMEM((groups - 1, lw, width), BF16),
            pltpu.VMEM((shares // 2, 2, block, latent), F32),
            pltpu.VMEM((shares // 2, block, latent), F32),
            pltpu.VMEM((shares // 2, block, latent), BF16),
            pltpu.VMEM((shares // 2, block, latent), BF16),
            pltpu.VMEM((shares // 2, 2, block, wide), F32),
            pltpu.VMEM((shares // 2, block, wide), F32),
            pltpu.VMEM((shares // 2, block, wide), BF16),
            pltpu.VMEM((shares // 2, block, wide), BF16),
            pltpu.VMEM((slots, wide), BF16),
            pltpu.SemaphoreType.DMA((len(ins),)),
            pltpu.SemaphoreType.DMA((9, 2, groups)),
            pltpu.SemaphoreType.DMA((8, 2, shares // 2)),
        ],
        compiler_params=pltpu.CompilerParams(
            collective_id=0, has_side_effects=True, vmem_limit_bytes=60 * 1024 * 1024
        ),
    )(*ins)
    outs = (
        jax.ShapeDtypeStruct((tokens, width), BF16),
        jax.ShapeDtypeStruct((lw, width), F32),
        jax.ShapeDtypeStruct((lw, width), F32),
        jax.ShapeDtypeStruct(ids_t.shape, F32),
        jax.ShapeDtypeStruct((ff, latent), F32),
        jax.ShapeDtypeStruct((ff, latent), F32),
    )
    input_grad, down_grad, up_grad, gate_grad, in_grad, out_grad = pl.pallas_call(
        functools.partial(outputs_kernel, groups, pad),
        out_shape=outs,
        in_specs=[hbm] * 11,
        out_specs=[hbm] * 6,
        scratch_shapes=[
            pltpu.VMEM(a.shape, a.dtype) for a in (*between, ids_t, down_proj)
        ]
        + [
            pltpu.VMEM(outs[n].shape, outs[n].dtype) for n in (0, 1, 3, 4, 5)
        ]
        + [pltpu.SemaphoreType.DMA((6,)), pltpu.SemaphoreType.DMA((11,))],
        compiler_params=pltpu.CompilerParams(vmem_limit_bytes=60 * 1024 * 1024),
    )(*between, ids_t, down_proj)
    return (input_grad, down_grad, up_grad, gate_grad.T, in_grad.T[None], out_grad[None])


def padded_rows(tokens):
    return -(-(tokens * 3 // 32) // (2 * ROWS)) * 2 * ROWS


def fits(layer_input, latent_saved, expert_in):
    groups = lax.axis_size("expert")
    shares = lax.axis_size("hidden")
    slots = groups * padded_rows(layer_input.shape[0])
    return (
        expert_in.shape[0] == 1
        and shares % 2 == 0
        and slots % (ROWS * shares) == 0
        and slots % LANES == 0
        and latent_saved.shape[1] % (LANES * groups) == 0
        and layer_input.shape[1] % LANES == 0
    )


def per_device(*arrays):
    run = fused if fits(arrays[0], arrays[2], arrays[8]) else on_device
    return run(*arrays)


def slot_layout(table, groups, local_count):
    tokens_here = table.shape[0]
    return table.T.reshape(groups, local_count, tokens_here).transpose(1, 0, 2)[:, :, None, :]


def on_device(
    layer_input,
    output_grad,
    latent_saved,
    combined_saved,
    expert_ids,
    gate_values,
    down_proj,
    up_proj,
    expert_in,
    expert_out,
):
    groups = lax.axis_size("expert")
    shares = lax.axis_size("hidden")
    tokens_here = layer_input.shape[0]
    latent_width = latent_saved.shape[1]
    local_count = expert_in.shape[0]
    capacity = tokens_here * 3 // 32
    live_count = local_count * groups
    slot_total = local_count * groups * capacity
    part_width = latent_width // shares
    partial_cot = jnp.einsum("td,ld->tl", output_grad, up_proj, preferred_element_type=jnp.float32)
    member = expert_ids[:, :, None] == jnp.arange(live_count, dtype=jnp.int32)[None, None, :]
    per_token = jnp.sum(member.astype(jnp.int32), axis=1)
    token_iota = jnp.arange(tokens_here, dtype=jnp.int32)
    earlier = (token_iota[None, :] < token_iota[:, None]).astype(jnp.bfloat16)
    before = jnp.dot(
        earlier, per_token.astype(jnp.bfloat16), preferred_element_type=jnp.float32
    ).astype(jnp.int32)
    gate_token = jnp.sum(
        jnp.where(member, gate_values.astype(jnp.float32)[:, :, None], 0.0), axis=1
    )
    rank_iota = jnp.arange(capacity, dtype=jnp.int32)[None, None, :, None]
    hit_slot = (slot_layout(per_token, groups, local_count) == 1) & (
        slot_layout(before, groups, local_count) == rank_iota
    )
    gate_slot = jnp.sum(
        jnp.where(hit_slot, slot_layout(gate_token, groups, local_count), 0.0), axis=3
    )
    gate_send = gate_slot.astype(jnp.bfloat16)
    dispatch_bf = hit_slot.astype(jnp.bfloat16).reshape(slot_total, tokens_here)
    cot_part = lax.psum_scatter(partial_cot, "hidden", scatter_dimension=1, tiled=True).astype(
        jnp.bfloat16
    )
    latent_part = lax.dynamic_slice_in_dim(
        latent_saved, lax.axis_index("hidden") * part_width, part_width, 1
    )
    cot_rows = jnp.dot(dispatch_bf, cot_part, preferred_element_type=jnp.float32).astype(
        jnp.bfloat16
    )
    latent_rows = jnp.dot(dispatch_bf, latent_part, preferred_element_type=jnp.float32).astype(
        jnp.bfloat16
    )
    cot_piece, latent_piece, gate_recv = (
        lax.all_to_all(
            cot_rows.reshape(local_count, groups, capacity, part_width),
            "expert",
            split_axis=1,
            concat_axis=1,
            tiled=True,
        ),
        lax.all_to_all(
            latent_rows.reshape(local_count, groups, capacity, part_width),
            "expert",
            split_axis=1,
            concat_axis=1,
            tiled=True,
        ),
        lax.all_to_all(gate_send, "expert", split_axis=1, concat_axis=1, tiled=True),
    )
    cot_recv, latent_recv = (
        lax.all_gather(cot_piece, "hidden", axis=3, tiled=True),
        lax.all_gather(latent_piece, "hidden", axis=3, tiled=True),
    )
    row_count = groups * capacity
    cot_block = cot_recv.reshape(local_count, row_count, latent_width)
    latent_block = latent_recv.reshape(local_count, row_count, latent_width)
    gate_block = gate_recv.reshape(local_count, row_count).astype(jnp.float32)
    pre_act = jnp.einsum(
        "erl,elf->erf", latent_block, expert_in, preferred_element_type=jnp.float32
    )
    relu_out = jnp.maximum(pre_act, 0.0)
    back_proj = jnp.einsum(
        "erl,efl->erf", cot_block, expert_out, preferred_element_type=jnp.float32
    )
    gate_part = jnp.sum(back_proj * relu_out * relu_out, axis=2)
    scaled_act = (gate_block[:, :, None] * relu_out * relu_out).astype(jnp.bfloat16)
    pre_grad = (2.0 * gate_block[:, :, None] * relu_out * back_proj).astype(jnp.bfloat16)
    expert_out_grad = jnp.einsum(
        "erf,erl->efl", scaled_act, cot_block, preferred_element_type=jnp.float32
    )
    expert_in_grad = jnp.einsum(
        "erl,erf->elf", latent_block, pre_grad, preferred_element_type=jnp.float32
    )
    latent_back = jnp.einsum(
        "erf,elf->erl", pre_grad, expert_in, preferred_element_type=jnp.float32
    )
    latent_back = latent_back.reshape(local_count, groups, capacity, latent_width)
    gate_part = gate_part.reshape(local_count, groups, capacity)
    dispatch_full = hit_slot.astype(jnp.float32)
    dispatch_flat = dispatch_full.reshape(slot_total, tokens_here)
    rows_home, gate_home = (
        lax.all_to_all(latent_back, "expert", split_axis=1, concat_axis=1, tiled=True),
        lax.all_to_all(gate_part, "expert", split_axis=1, concat_axis=1, tiled=True),
    )
    token_sums = jnp.dot(
        dispatch_flat.T,
        rows_home.reshape(slot_total, latent_width),
        precision=lax.Precision.HIGHEST,
        preferred_element_type=jnp.float32,
    )
    by_expert = jnp.sum(dispatch_full * gate_home[:, :, :, None], axis=2)
    by_expert = by_expert.transpose(2, 1, 0).reshape(tokens_here, live_count)
    gate_local = jnp.sum(jnp.where(member, by_expert[:, None, :], 0.0), axis=2)
    latent_grad, gate_grad = lax.psum((token_sums, gate_local), "hidden")
    latent_bf = latent_grad.astype(jnp.bfloat16)
    input_grad = jnp.dot(latent_bf, down_proj, preferred_element_type=jnp.float32).astype(
        jnp.bfloat16
    )
    down_term = jnp.einsum("tl,td->ld", latent_bf, layer_input, preferred_element_type=jnp.float32)
    up_term = jnp.einsum(
        "tl,td->ld", combined_saved, output_grad, preferred_element_type=jnp.float32
    )
    down_grad, up_grad = (
        lax.psum_scatter(down_term, "expert", scatter_dimension=0, tiled=True),
        lax.psum_scatter(up_term, "expert", scatter_dimension=0, tiled=True),
    )
    return (input_grad, down_grad, up_grad, gate_grad, expert_in_grad, expert_out_grad)


def solution(mesh):
    return jax.shard_map(
        per_device,
        mesh=mesh,
        in_specs=(
            P("expert", "hidden"),
            P("expert", "hidden"),
            P("expert", None),
            P("expert", None),
            P("expert", None),
            P("expert", None),
            P(None, "hidden"),
            P(None, "hidden"),
            P("expert", None, "hidden"),
            P("expert", "hidden", None),
        ),
        out_specs=(
            P("expert", "hidden"),
            P("expert", "hidden"),
            P("expert", "hidden"),
            P("expert", None),
            P("expert", None, "hidden"),
            P("expert", "hidden", None),
        ),
        check_vma=False,
    )
```

```python
import functools

import jax
import jax.numpy as jnp
from jax import lax
from jax.experimental import pallas as pl
from jax.experimental.pallas import tpu as pltpu
from jax.sharding import PartitionSpec as P

F32 = jnp.float32
BF16 = jnp.bfloat16
LANES = 128
ROWS = 16


def mm(a, b, ca, cb):
    return lax.dot_general(a, b, (((ca,), (cb,)), ((), ())), preferred_element_type=F32)


def rows_at(index, size):
    return pl.ds(pl.multiple_of(index * size, size), size)


def fused_kernel(
    groups,
    shares,
    pad,
    x_hbm,
    og_hbm,
    z_hbm,
    u_hbm,
    ids_hbm,
    gates_hbm,
    up_hbm,
    ein_hbm,
    eout_hbm,
    disp_out,
    scaled_out,
    pre_out,
    zb_out,
    cag_out,
    home_out,
    dn_out,
    x_out,
    ug_out,
    disp_ref,
    scaled_ref,
    pre_ref,
    zb_ref,
    cag,
    home,
    dn,
    x_r,
    ug_ref,
    x_ref,
    og_ref,
    z_ref,
    u_ref,
    ids_ref,
    gates_ref,
    up_ref,
    ein_ref,
    eout_ref,
    og_s,
    og_r,
    z_s,
    z_r,
    x_s,
    up_s,
    up_r,
    cf,
    ch,
    cs,
    cr,
    bf,
    bh,
    bs,
    br,
    bag,
    sems_in,
    sems_out,
    sems_e,
    sems_h,
):
    e = lax.axis_index("expert")
    h = lax.axis_index("hidden")
    tokens = ids_ref.shape[1]
    slots = groups * pad
    latent = z_ref.shape[1]
    block = slots // shares
    lw = latent // groups

    def expert_peer(j):
        return lax.rem(e + j, groups)

    pairs = shares // 2
    core = lax.rem(h, 2)
    line = h // 2
    sibling = line * 2 + 1 - core

    def line_peer(j):
        return lax.rem(line + j, pairs)

    def line_source(j):
        return lax.rem(line + (pairs - j), pairs)

    def to_expert(phase, j, src, dst):
        copy = pltpu.make_async_remote_copy(
            src_ref=src,
            dst_ref=dst,
            send_sem=sems_e.at[phase, 0, j],
            recv_sem=sems_e.at[phase, 1, j],
            device_id=(expert_peer(j), h),
            device_id_type=pl.DeviceIdType.MESH,
        )
        copy.start()
        return copy

    def to_hidden(phase, j, peer, src, dst):
        copy = pltpu.make_async_remote_copy(
            src_ref=src,
            dst_ref=dst,
            send_sem=sems_h.at[phase, 0, j],
            recv_sem=sems_h.at[phase, 1, j],
            device_id=(e, peer),
            device_id_type=pl.DeviceIdType.MESH,
        )
        copy.start()
        return copy

    def to_sibling(phase, j, src, dst):
        copy = pltpu.make_async_remote_copy(
            src_ref=src,
            dst_ref=dst,
            send_sem=sems_e.at[phase, 0, j],
            recv_sem=sems_e.at[phase, 1, j],
            device_id=(e, sibling),
            device_id_type=pl.DeviceIdType.MESH,
        )
        copy.start()
        return copy

    def expert_source(j):
        return lax.rem(e + (groups - j), groups)

    def swap_halves(phase, full, half):
        return to_hidden(phase, 0, sibling, full.at[:, 1 - core], half)

    def scatter_start(phase, swap, full, half, sends, lands):
        swap.wait_recv()
        sends[...] = (full[:, core] + half[...]).astype(BF16)
        return [
            to_hidden(
                phase, j, line_peer(j) * 2 + core, sends.at[line_peer(j)], lands.at[line]
            )
            for j in range(1, pairs)
        ]

    def scatter_sums(copies, full, half, lands):
        total = full[line, core] + half[line]
        for j in range(1, pairs):
            copies[j - 1].wait_recv()
            total = total + lands[line_source(j)].astype(F32)
        return total.astype(BF16)

    def gather_blocks(phase, full):
        mine = full.at[rows_at(h, block)]
        copies = [
            to_hidden(phase, j, line_peer(j) * 2 + core, mine, mine)
            for j in range(1, pairs)
        ]
        shared = [to_hidden(phase + 1, 0, sibling, mine, mine)]
        for j in range(1, pairs):
            copies[j - 1].wait_recv()
            theirs = full.at[rows_at(line_source(j) * 2 + core, block)]
            shared.append(to_hidden(phase + 1, j, sibling, theirs, theirs))
        return copies, shared

    stores = []

    def store(src, dst):
        copy = pltpu.make_async_copy(src, dst, sems_out.at[len(stores)])
        copy.start()
        stores.append(copy)

    sources = (ids_hbm, gates_hbm, og_hbm, z_hbm, up_hbm, ein_hbm, x_hbm, u_hbm, eout_hbm)
    targets = (ids_ref, gates_ref, og_ref, z_ref, up_ref, ein_ref, x_ref, u_ref, eout_ref)
    loads = [
        pltpu.make_async_copy(src, dst, sems_in.at[n])
        for n, (src, dst) in enumerate(zip(sources, targets))
    ]
    for load in loads:
        load.start()
    ids_in, gates_in, og_in, z_in, up_in, ein_in, x_in, u_in, eout_in = loads

    barrier = pltpu.get_barrier_semaphore()
    for j in range(1, groups):
        pl.semaphore_signal(
            barrier,
            inc=1,
            device_id=(expert_peer(j), h),
            device_id_type=pl.DeviceIdType.MESH,
        )
    for peer in [sibling] + [line_peer(j) * 2 + core for j in range(1, pairs)]:
        pl.semaphore_signal(
            barrier,
            inc=1,
            device_id=(e, peer),
            device_id_type=pl.DeviceIdType.MESH,
        )

    row_t = lax.broadcasted_iota(jnp.int32, (tokens, tokens), 0)
    col_t = lax.broadcasted_iota(jnp.int32, (tokens, tokens), 1)
    earlier = jnp.where(row_t < col_t, 1.0, 0.0).astype(BF16)
    ids_in.wait()
    gates_in.wait()
    ids = ids_ref[...]
    gates = gates_ref[...].astype(F32)
    member_rows = []
    gate_rows = []
    for n in range(groups):
        hit = ids == n
        member_rows.append(jnp.sum(jnp.where(hit, 1.0, 0.0), axis=0, keepdims=True))
        gate_rows.append(jnp.sum(jnp.where(hit, gates, 0.0), axis=0, keepdims=True))
    member = jnp.concatenate(
        [jnp.broadcast_to(row, (pad, tokens)) for row in member_rows], axis=0
    )
    gate_token = jnp.concatenate(
        [jnp.broadcast_to(row, (pad, tokens)) for row in gate_rows], axis=0
    )
    before = mm(member.astype(BF16), earlier, 1, 0)
    slot = lax.broadcasted_iota(jnp.int32, (slots, tokens), 0)
    rank = lax.rem(slot, pad).astype(F32)
    chosen = jnp.where(before == rank, member, 0.0)
    disp = chosen.astype(BF16)
    disp_ref[...] = disp
    og_in.wait()

    og_s[...] = mm(disp, og_ref[...], 1, 0).astype(BF16).reshape(og_s.shape)
    pl.semaphore_wait(barrier, groups + pairs - 1)
    og_c = [
        to_expert(0, j, og_s.at[expert_peer(j)], og_r.at[e]) for j in range(1, groups)
    ]
    z_in.wait()
    z_s[:, :, 0:latent] = mm(disp, z_ref[...], 1, 0).astype(BF16).reshape(groups, pad, latent)
    gate_col = jnp.sum(chosen * gate_token, axis=1, keepdims=True)
    z_s[:, :, latent : latent + LANES] = (
        jnp.broadcast_to(gate_col, (slots, LANES)).astype(BF16).reshape(groups, pad, LANES)
    )
    my_rows = rows_at(core, pad // 2)
    z_c = [
        to_expert(1, j, z_s.at[expert_peer(j), my_rows], z_r.at[e, my_rows])
        for j in range(1, groups)
    ]
    og_r[e] = og_s[e]
    z_r[e] = z_s[e]
    x_in.wait()
    x_s[...] = mm(disp, x_ref[...], 1, 0).astype(BF16).reshape(x_s.shape)
    x_r[:, rows_at(e, pad), :] = x_s[...]
    u_in.wait()
    for j in range(1, groups):
        up_s[j - 1] = mm(
            u_ref[:, rows_at(expert_peer(j), lw)], og_ref[...], 0, 0
        ).astype(BF16)
    ug_ref[...] = mm(u_ref[:, rows_at(e, lw)], og_ref[...], 0, 0)

    for c in og_c:
        c.wait_recv()
    up_in.wait()
    cot_part = mm(og_r[...].reshape(slots, og_ref.shape[1]), up_ref[...], 1, 1)
    cf[...] = cot_part.reshape(cf.shape)
    cot_swap = swap_halves(0, cf, ch)
    crs = scatter_start(1, cot_swap, cf, ch, cs, cr)
    z_f = []
    for j in range(1, groups):
        z_c[j - 1].wait_recv()
        landed = z_r.at[expert_source(j), my_rows]
        z_f.append(to_sibling(6, j, landed, landed))
    x_c = [
        to_expert(2, j, x_s, x_r.at[:, rows_at(e, pad), :]) for j in range(1, groups)
    ]
    up_c = [to_expert(3, j, up_s.at[j - 1], up_r.at[j - 1]) for j in range(1, groups)]
    for c in z_f:
        c.wait_recv()
    zb = z_r[:, :, 0:latent].reshape(slots, latent)
    gate_b = z_r[:, :, latent : latent + LANES].astype(F32).reshape(slots, LANES)[:, 0:1]
    zb_ref[...] = zb
    ein_in.wait()
    act = jnp.maximum(mm(zb, ein_ref[...], 1, 1), 0.0)
    square = act * act
    scaled_ref[...] = (gate_b * square).astype(BF16)
    eout_in.wait()
    cag[rows_at(h, block), :] = scatter_sums(crs, cf, ch, cr)
    cagc, cags = gather_blocks(2, cag)
    for c in cags:
        c.wait_recv()

    cotb = cag[...]
    back = mm(cotb, eout_ref[...], 1, 1)
    gate_part = jnp.sum(back * square, axis=1, keepdims=True)
    pre_grad = ((2.0 * gate_b) * act * back).astype(BF16)
    pre_ref[...] = pre_grad
    part = mm(pre_grad, ein_ref[...], 1, 0)
    gate_wide = jnp.broadcast_to(gate_part, (slots, LANES))
    bf[:, :, :, 0:latent] = part.reshape(pairs, 2, block, latent)
    bf[:, :, :, latent : latent + LANES] = gate_wide.reshape(pairs, 2, block, LANES)
    back_swap = swap_halves(4, bf, bh)
    store(disp_ref, disp_out)
    store(scaled_ref, scaled_out)
    store(pre_ref, pre_out)
    store(zb_ref, zb_out)
    store(cag, cag_out)
    brs = scatter_start(5, back_swap, bf, bh, bs, br)
    bag[rows_at(h, block), :] = scatter_sums(brs, bf, bh, br)
    bagc, bags = gather_blocks(6, bag)
    for c in bags:
        c.wait_recv()

    half_pad = pad // 2
    my_half = rows_at(core, slots // 2)
    home_c = [
        to_expert(
            4,
            j,
            bag.at[rows_at(expert_peer(j) * 2 + core, half_pad)],
            home.at[rows_at(e * 2 + core, half_pad)],
        )
        for j in range(1, groups)
    ]
    dn_c = [
        to_expert(5, j, bag.at[my_half, rows_at(expert_peer(j), lw)], dn.at[e, my_half])
        for j in range(1, groups)
    ]
    home[rows_at(e, pad), :] = bag[rows_at(e, pad), :]
    dn[e] = bag[:, rows_at(e, lw)]
    for j in range(1, groups):
        up_c[j - 1].wait_recv()
        ug_ref[...] += up_r[j - 1].astype(F32)
    for c in x_c:
        c.wait_recv()
    store(ug_ref, ug_out)
    store(x_r, x_out)
    last_f = []
    for j in range(1, groups):
        home_c[j - 1].wait_recv()
        landed = home.at[rows_at(expert_source(j) * 2 + core, half_pad)]
        last_f.append(to_sibling(7, j, landed, landed))
    for j in range(1, groups):
        dn_c[j - 1].wait_recv()
        landed = dn.at[expert_source(j), my_half]
        last_f.append(to_sibling(8, j, landed, landed))
    for c in last_f:
        c.wait_recv()
    store(home, home_out)
    store(dn, dn_out)
    for c in stores:
        c.wait()
    sent = og_c + z_c + [cot_swap] + crs + x_c + up_c + cagc + cags
    sent += [back_swap] + brs + bagc + bags + home_c + dn_c + z_f + last_f
    for c in sent:
        c.wait_send()


def outputs_kernel(
    groups,
    pad,
    *refs,
):
    sources, refs = refs[:11], refs[11:]
    (ig_hbm, dg_hbm, ug_hbm, gg_hbm, eig_hbm, eog_hbm), refs = refs[:6], refs[6:]
    targets, refs = refs[:11], refs[11:]
    ig_v, dg_v, gg_v, eig_v, eog_v, sems, sems_in = refs
    (
        disp_ref,
        scaled_ref,
        pre_ref,
        zb_ref,
        cot_ref,
        home_ref,
        dn_ref,
        x_ref,
        ug_ref,
        ids_ref,
        down_ref,
    ) = targets
    loads = [
        pltpu.make_async_copy(src, dst, sems_in.at[n])
        for n, (src, dst) in enumerate(zip(sources, targets))
    ]
    order = (1, 4, 2, 3, 8, 6, 7, 0, 5, 10, 9)
    for n in order:
        loads[n].start()
    slots = groups * pad
    latent = cot_ref.shape[1]
    stores = []

    def store(src, dst):
        copy = pltpu.make_async_copy(src, dst, sems.at[len(stores)])
        copy.start()
        stores.append(copy)

    loads[1].wait()
    loads[4].wait()
    eog_v[...] = mm(scaled_ref[...], cot_ref[...], 0, 0)
    store(eog_v, eog_hbm)
    loads[2].wait()
    loads[3].wait()
    eig_v[...] = mm(pre_ref[...], zb_ref[...], 0, 0)
    store(eig_v, eig_hbm)
    loads[8].wait()
    store(ug_ref, ug_hbm)
    loads[6].wait()
    loads[7].wait()
    dg_v[...] = mm(
        dn_ref[...].reshape(groups * slots, dn_ref.shape[2]),
        x_ref[...].reshape(groups * slots, x_ref.shape[2]),
        0,
        0,
    )
    store(dg_v, dg_hbm)
    for n in (0, 5, 10, 9):
        loads[n].wait()
    disp = disp_ref[...]
    latent_grad = mm(disp, home_ref[:, 0:latent], 0, 0).astype(BF16)
    ig_v[...] = mm(latent_grad, down_ref[...], 1, 0).astype(BF16)
    store(ig_v, ig_hbm)
    by_slot = home_ref[:, latent : latent + LANES].astype(F32)[:, 0:1] * disp.astype(F32)
    ids = ids_ref[...]
    gate_out = jnp.zeros(ids.shape, F32)
    for n in range(groups):
        by_token = jnp.sum(by_slot[n * pad : (n + 1) * pad], axis=0, keepdims=True)
        gate_out = jnp.where(ids == n, by_token, gate_out)
    gg_v[...] = gate_out
    store(gg_v, gg_hbm)
    for copy in stores:
        copy.wait()


def fused(
    layer_input,
    output_grad,
    latent_saved,
    combined_saved,
    expert_ids,
    gate_values,
    down_proj,
    up_proj,
    expert_in,
    expert_out,
):
    groups = lax.axis_size("expert")
    shares = lax.axis_size("hidden")
    tokens, width = layer_input.shape
    latent = latent_saved.shape[1]
    ff = expert_in.shape[2]
    pad = padded_rows(tokens)
    slots = groups * pad
    block = slots // shares
    wide = latent + LANES
    lw = latent // groups
    hbm = pl.BlockSpec(memory_space=pltpu.HBM)
    ids_t = expert_ids.T
    ins = (
        layer_input,
        output_grad,
        latent_saved,
        combined_saved,
        ids_t,
        gate_values.T,
        up_proj,
        expert_in[0].T,
        expert_out[0],
    )
    middle = (
        jax.ShapeDtypeStruct((slots, tokens), BF16),
        jax.ShapeDtypeStruct((slots, ff), BF16),
        jax.ShapeDtypeStruct((slots, ff), BF16),
        jax.ShapeDtypeStruct((slots, latent), BF16),
        jax.ShapeDtypeStruct((slots, latent), BF16),
        jax.ShapeDtypeStruct((slots, wide), BF16),
        jax.ShapeDtypeStruct((groups, slots, lw), BF16),
        jax.ShapeDtypeStruct((groups, slots, width), BF16),
        jax.ShapeDtypeStruct((lw, width), F32),
    )
    between = pl.pallas_call(
        functools.partial(fused_kernel, groups, shares, pad),
        out_shape=middle,
        in_specs=[hbm] * len(ins),
        out_specs=[hbm] * len(middle),
        scratch_shapes=[pltpu.VMEM(a.shape, a.dtype) for a in middle + ins]
        + [
            pltpu.VMEM((groups, pad, width), BF16),
            pltpu.VMEM((groups, pad, width), BF16),
            pltpu.VMEM((groups, pad, wide), BF16),
            pltpu.VMEM((groups, pad, wide), BF16),
            pltpu.VMEM((groups, pad, width), BF16),
            pltpu.VMEM((groups - 1, lw, width), BF16),
            pltpu.VMEM((groups - 1, lw, width), BF16),
            pltpu.VMEM((shares // 2, 2, block, latent), F32),
            pltpu.VMEM((shares // 2, block, latent), F32),
            pltpu.VMEM((shares // 2, block, latent), BF16),
            pltpu.VMEM((shares // 2, block, latent), BF16),
            pltpu.VMEM((shares // 2, 2, block, wide), F32),
            pltpu.VMEM((shares // 2, block, wide), F32),
            pltpu.VMEM((shares // 2, block, wide), BF16),
            pltpu.VMEM((shares // 2, block, wide), BF16),
            pltpu.VMEM((slots, wide), BF16),
            pltpu.SemaphoreType.DMA((len(ins),)),
            pltpu.SemaphoreType.DMA((len(middle),)),
            pltpu.SemaphoreType.DMA((9, 2, groups)),
            pltpu.SemaphoreType.DMA((8, 2, shares // 2)),
        ],
        compiler_params=pltpu.CompilerParams(
            collective_id=0, has_side_effects=True, vmem_limit_bytes=60 * 1024 * 1024
        ),
    )(*ins)
    outs = (
        jax.ShapeDtypeStruct((tokens, width), BF16),
        jax.ShapeDtypeStruct((lw, width), F32),
        jax.ShapeDtypeStruct((lw, width), F32),
        jax.ShapeDtypeStruct(ids_t.shape, F32),
        jax.ShapeDtypeStruct((ff, latent), F32),
        jax.ShapeDtypeStruct((ff, latent), F32),
    )
    input_grad, down_grad, up_grad, gate_grad, in_grad, out_grad = pl.pallas_call(
        functools.partial(outputs_kernel, groups, pad),
        out_shape=outs,
        in_specs=[hbm] * 11,
        out_specs=[hbm] * 6,
        scratch_shapes=[
            pltpu.VMEM(a.shape, a.dtype) for a in (*between, ids_t, down_proj)
        ]
        + [
            pltpu.VMEM(outs[n].shape, outs[n].dtype) for n in (0, 1, 3, 4, 5)
        ]
        + [pltpu.SemaphoreType.DMA((6,)), pltpu.SemaphoreType.DMA((11,))],
        compiler_params=pltpu.CompilerParams(vmem_limit_bytes=60 * 1024 * 1024),
    )(*between, ids_t, down_proj)
    return (input_grad, down_grad, up_grad, gate_grad.T, in_grad.T[None], out_grad[None])


def padded_rows(tokens):
    return -(-(tokens * 3 // 32) // (2 * ROWS)) * 2 * ROWS


def fits(layer_input, latent_saved, expert_in):
    groups = lax.axis_size("expert")
    shares = lax.axis_size("hidden")
    slots = groups * padded_rows(layer_input.shape[0])
    return (
        expert_in.shape[0] == 1
        and shares % 2 == 0
        and slots % (ROWS * shares) == 0
        and slots % LANES == 0
        and latent_saved.shape[1] % (LANES * groups) == 0
        and layer_input.shape[1] % LANES == 0
    )


def per_device(*arrays):
    run = fused if fits(arrays[0], arrays[2], arrays[8]) else on_device
    return run(*arrays)


def slot_layout(table, groups, local_count):
    tokens_here = table.shape[0]
    return table.T.reshape(groups, local_count, tokens_here).transpose(1, 0, 2)[:, :, None, :]


def on_device(
    layer_input,
    output_grad,
    latent_saved,
    combined_saved,
    expert_ids,
    gate_values,
    down_proj,
    up_proj,
    expert_in,
    expert_out,
):
    groups = lax.axis_size("expert")
    shares = lax.axis_size("hidden")
    tokens_here = layer_input.shape[0]
    latent_width = latent_saved.shape[1]
    local_count = expert_in.shape[0]
    capacity = tokens_here * 3 // 32
    live_count = local_count * groups
    slot_total = local_count * groups * capacity
    part_width = latent_width // shares
    partial_cot = jnp.einsum("td,ld->tl", output_grad, up_proj, preferred_element_type=jnp.float32)
    member = expert_ids[:, :, None] == jnp.arange(live_count, dtype=jnp.int32)[None, None, :]
    per_token = jnp.sum(member.astype(jnp.int32), axis=1)
    token_iota = jnp.arange(tokens_here, dtype=jnp.int32)
    earlier = (token_iota[None, :] < token_iota[:, None]).astype(jnp.bfloat16)
    before = jnp.dot(
        earlier, per_token.astype(jnp.bfloat16), preferred_element_type=jnp.float32
    ).astype(jnp.int32)
    gate_token = jnp.sum(
        jnp.where(member, gate_values.astype(jnp.float32)[:, :, None], 0.0), axis=1
    )
    rank_iota = jnp.arange(capacity, dtype=jnp.int32)[None, None, :, None]
    hit_slot = (slot_layout(per_token, groups, local_count) == 1) & (
        slot_layout(before, groups, local_count) == rank_iota
    )
    gate_slot = jnp.sum(
        jnp.where(hit_slot, slot_layout(gate_token, groups, local_count), 0.0), axis=3
    )
    gate_send = gate_slot.astype(jnp.bfloat16)
    dispatch_bf = hit_slot.astype(jnp.bfloat16).reshape(slot_total, tokens_here)
    cot_part = lax.psum_scatter(partial_cot, "hidden", scatter_dimension=1, tiled=True).astype(
        jnp.bfloat16
    )
    latent_part = lax.dynamic_slice_in_dim(
        latent_saved, lax.axis_index("hidden") * part_width, part_width, 1
    )
    cot_rows = jnp.dot(dispatch_bf, cot_part, preferred_element_type=jnp.float32).astype(
        jnp.bfloat16
    )
    latent_rows = jnp.dot(dispatch_bf, latent_part, preferred_element_type=jnp.float32).astype(
        jnp.bfloat16
    )
    cot_piece, latent_piece, gate_recv = (
        lax.all_to_all(
            cot_rows.reshape(local_count, groups, capacity, part_width),
            "expert",
            split_axis=1,
            concat_axis=1,
            tiled=True,
        ),
        lax.all_to_all(
            latent_rows.reshape(local_count, groups, capacity, part_width),
            "expert",
            split_axis=1,
            concat_axis=1,
            tiled=True,
        ),
        lax.all_to_all(gate_send, "expert", split_axis=1, concat_axis=1, tiled=True),
    )
    cot_recv, latent_recv = (
        lax.all_gather(cot_piece, "hidden", axis=3, tiled=True),
        lax.all_gather(latent_piece, "hidden", axis=3, tiled=True),
    )
    row_count = groups * capacity
    cot_block = cot_recv.reshape(local_count, row_count, latent_width)
    latent_block = latent_recv.reshape(local_count, row_count, latent_width)
    gate_block = gate_recv.reshape(local_count, row_count).astype(jnp.float32)
    pre_act = jnp.einsum(
        "erl,elf->erf", latent_block, expert_in, preferred_element_type=jnp.float32
    )
    relu_out = jnp.maximum(pre_act, 0.0)
    back_proj = jnp.einsum(
        "erl,efl->erf", cot_block, expert_out, preferred_element_type=jnp.float32
    )
    gate_part = jnp.sum(back_proj * relu_out * relu_out, axis=2)
    scaled_act = (gate_block[:, :, None] * relu_out * relu_out).astype(jnp.bfloat16)
    pre_grad = (2.0 * gate_block[:, :, None] * relu_out * back_proj).astype(jnp.bfloat16)
    expert_out_grad = jnp.einsum(
        "erf,erl->efl", scaled_act, cot_block, preferred_element_type=jnp.float32
    )
    expert_in_grad = jnp.einsum(
        "erl,erf->elf", latent_block, pre_grad, preferred_element_type=jnp.float32
    )
    latent_back = jnp.einsum(
        "erf,elf->erl", pre_grad, expert_in, preferred_element_type=jnp.float32
    )
    latent_back = latent_back.reshape(local_count, groups, capacity, latent_width)
    gate_part = gate_part.reshape(local_count, groups, capacity)
    dispatch_full = hit_slot.astype(jnp.float32)
    dispatch_flat = dispatch_full.reshape(slot_total, tokens_here)
    rows_home, gate_home = (
        lax.all_to_all(latent_back, "expert", split_axis=1, concat_axis=1, tiled=True),
        lax.all_to_all(gate_part, "expert", split_axis=1, concat_axis=1, tiled=True),
    )
    token_sums = jnp.dot(
        dispatch_flat.T,
        rows_home.reshape(slot_total, latent_width),
        precision=lax.Precision.HIGHEST,
        preferred_element_type=jnp.float32,
    )
    by_expert = jnp.sum(dispatch_full * gate_home[:, :, :, None], axis=2)
    by_expert = by_expert.transpose(2, 1, 0).reshape(tokens_here, live_count)
    gate_local = jnp.sum(jnp.where(member, by_expert[:, None, :], 0.0), axis=2)
    latent_grad, gate_grad = lax.psum((token_sums, gate_local), "hidden")
    latent_bf = latent_grad.astype(jnp.bfloat16)
    input_grad = jnp.dot(latent_bf, down_proj, preferred_element_type=jnp.float32).astype(
        jnp.bfloat16
    )
    down_term = jnp.einsum("tl,td->ld", latent_bf, layer_input, preferred_element_type=jnp.float32)
    up_term = jnp.einsum(
        "tl,td->ld", combined_saved, output_grad, preferred_element_type=jnp.float32
    )
    down_grad, up_grad = (
        lax.psum_scatter(down_term, "expert", scatter_dimension=0, tiled=True),
        lax.psum_scatter(up_term, "expert", scatter_dimension=0, tiled=True),
    )
    return (input_grad, down_grad, up_grad, gate_grad, expert_in_grad, expert_out_grad)


def solution(mesh):
    return jax.shard_map(
        per_device,
        mesh=mesh,
        in_specs=(
            P("expert", "hidden"),
            P("expert", "hidden"),
            P("expert", None),
            P("expert", None),
            P("expert", None),
            P("expert", None),
            P(None, "hidden"),
            P(None, "hidden"),
            P("expert", None, "hidden"),
            P("expert", "hidden", None),
        ),
        out_specs=(
            P("expert", "hidden"),
            P("expert", "hidden"),
            P("expert", "hidden"),
            P("expert", None),
            P("expert", None, "hidden"),
            P("expert", "hidden", None),
        ),
        check_vma=False,
    )
```
